128 devices in a mesh: ctx: 8 (over x_lo, z), head: 16 (over x_hi, y, core).
Axes of the slice: x: 4 (x_hi: 2, x_lo: 2; x = x_hi * 2 + x_lo), y: 4, z: 4, core: 2. Of those that a mesh axis runs over, the one named last changes fastest.
Arguments:
- q_nope: bfloat16 [2048, 16384], P('ctx', 'head'), may hold values from -6 to 6
- q_rope: bfloat16 [2048, 8192], P('ctx', 'head'), may hold values from -8 to 8
- latent: bfloat16 [2048, 512], P('ctx'), may hold values from -6 to 6
- latent_gain: bfloat16 [512], replicated, may hold values from 0.25 to 1.75
- k_rope_t: bfloat16 [64, 2048], P(None, 'ctx'), may hold values from -8 to 8
- w_uk: bfloat16 [16384, 512], P('head'), may hold values from -0.25 to 0.25
- w_uv: bfloat16 [16384, 512], P('head'), may hold values from -0.25 to 0.25
- d_out: bfloat16 [2048, 16384], P('ctx', 'head'), may hold values from -6 to 6
- group_ids: int32 [2048], P('ctx'), may hold values from 0 to 1, as said below
- comp_ids: int32 [2048], P('ctx'), may hold values from 0 to 8, as said below
- comp_lengths: int32 [2, 8], replicated, may hold values from 64 to 112, as said below
Outputs:
- attn_out: bfloat16 [2048, 16384], P('ctx', 'head')
- d_q_nope: bfloat16 [2048, 16384], P('ctx', 'head')
- d_q_rope: bfloat16 [2048, 8192], P('ctx', 'head')
- d_latent: bfloat16 [2048, 512], P('ctx')
- d_k_rope_t: bfloat16 [64, 2048], P(None, 'ctx')
- d_w_uk: bfloat16 [16384, 512], P('head')
- d_w_uv: bfloat16 [16384, 512], P('head')
The draws below stay inside these ranges and needn't reach their ends.
Inputs may be any that keep to these rules, and one draw needn't show every extreme that they name: `group_ids`: non-decreasing; every one of the 2 groups holds tokens. `comp_ids`: each group opens with a prompt of 2 or more tokens (id 0), then completions 1 to 8 follow in order, each of 64 to 112 tokens. comp_lengths[g, k] is the number of tokens with group g and completion k + 1.
All inputs are finite; a program needn't handle non-finite values.
Results may differ from the reference program's by a relative error of at most 0.025.
Values may be sent and summed in bfloat16 or wider, within the bound.
No kernel may reach another device: no remote copies, remote signals or barrier semaphores. Data moves between devices by JAX's collectives and lax.ppermute only.
A program may use at most 128 MiB of HBM per device.

```python
import math
import jax
import jax.numpy as jnp
from jax import lax

D_LAT = 512
D_ROPE = 64
D_NOPE = 128
D_V = 128
H = 128
GROUPS = 2
COMP = 8
TOKENS = 2048


def pack_layout(key):
    key_group, key_comp = jax.random.split(jax.random.fold_in(key, 11), 2)
    least = TOKENS // (2 * GROUPS * COMP)
    most = TOKENS * 7 // (8 * GROUPS * COMP)
    lengths = jax.random.randint(key_comp, (GROUPS, COMP), least, most + 1)
    lengths = lengths.at[0, 0].set(least)
    lengths = lengths.at[0, 1].set(most)
    comp_total = jnp.sum(lengths, axis=1)
    remaining = TOKENS - jnp.sum(comp_total)
    shares = jax.random.randint(key_group, (GROUPS,), 3, 6)
    prompt = 2 + (remaining - 2 * GROUPS) * shares // jnp.sum(shares)
    prompt = prompt.at[-1].add(remaining - jnp.sum(prompt))
    group_len = prompt + comp_total
    group_start = jnp.cumsum(group_len) - group_len
    comp_start = group_start[:, None] + prompt[:, None] + jnp.cumsum(lengths, axis=1) - lengths
    position = jnp.arange(TOKENS, dtype=jnp.int32)
    group_ids = jnp.sum(position[:, None] >= group_start[None, 1:], axis=1).astype(jnp.int32)
    member = group_ids[:, None, None] == jnp.arange(GROUPS, dtype=jnp.int32)[None, :, None]
    comp_ids = jnp.sum((position[:, None, None] >= comp_start[None]) & member, axis=(1, 2)).astype(jnp.int32)
    return (group_ids, comp_ids, lengths.astype(jnp.int32))


def draw_group_ids(key, part):
    return pack_layout(key)[0]


def draw_comp_ids(key, part):
    return pack_layout(key)[1]


def draw_comp_lengths(key, part):
    return pack_layout(key)[2]


def draw_q_rope(key, part):
    key = jax.random.fold_in(key, 3)
    values_f = jnp.clip(jax.random.normal(key, (TOKENS, H * D_ROPE), jnp.float32), -4.0, 4.0)
    return values_f.astype(jnp.bfloat16)


def draw_k_rope_t(key, part):
    key = jax.random.fold_in(key, 5)
    values_f = jnp.clip(jax.random.normal(key, (D_ROPE, TOKENS), jnp.float32), -4.0, 4.0)
    return values_f.astype(jnp.bfloat16)


def levels(rng, shape, cuts, smallest, largest):
    level, own = 1.0, jax.random.fold_in(rng, 6)
    for axis_at, blocks in cuts:
        steps = jnp.exp(jax.random.uniform(jax.random.fold_in(own, axis_at), (blocks,), jnp.float32, smallest / len(cuts), largest / len(cuts)))
        level = level * jnp.repeat(steps, shape[axis_at] // blocks).reshape([-1 if axis == axis_at else 1 for axis in range(len(shape))])
    return level


def bell_draw(key, shape, width, reach, cuts=(), kind=jnp.bfloat16):
    array = jax.random.normal(key, shape, jnp.float32) * width
    if len(cuts) > 0:
        array = levels(key, shape, cuts, -0.22, 0.18) * array
    return jnp.clip(array, min=-reach, max=reach).astype(kind)


def setup_inputs(seed: int = 0) -> dict:
    keys = jax.random.split(jax.random.key(seed), 12)
    return {
        "q_nope": bell_draw(keys[0], (TOKENS, H * D_NOPE), 1.0, 6.0, ((0, 8), (1, 16))),
        "q_rope": draw_q_rope(jax.random.fold_in(keys[11], 71), 0),
        "latent": bell_draw(keys[2], (TOKENS, D_LAT), 1.0, 6.0, ((0, 8),)),
        "latent_gain": jnp.clip(1.0 + 0.15 * jax.random.normal(keys[3], (D_LAT,), jnp.float32), 0.25, 1.75).astype(jnp.bfloat16),
        "k_rope_t": draw_k_rope_t(jax.random.fold_in(keys[11], 71), 0),
        "w_uk": bell_draw(keys[5], (H * D_NOPE, D_LAT), D_LAT ** -0.5, 0.25, ((0, 16),)),
        "w_uv": bell_draw(keys[6], (H * D_V, D_LAT), D_LAT ** -0.5, 0.25, ((0, 16),)),
        "d_out": bell_draw(keys[7], (TOKENS, H * D_V), 1.0, 6.0, ((0, 8), (1, 16))),
        "group_ids": draw_group_ids(jax.random.fold_in(keys[11], 71), 0),
        "comp_ids": draw_comp_ids(jax.random.fold_in(keys[11], 71), 0),
        "comp_lengths": draw_comp_lengths(jax.random.fold_in(keys[11], 71), 0),
    }


def token_weights(group_ids, comp_ids, comp_lengths):
    slot_index = group_ids * COMP + comp_ids - 1
    table = jnp.arange(GROUPS * COMP, dtype=jnp.int32)
    onehot = (slot_index[:, None] == table[None, :]) & (comp_ids[:, None] > 0)
    flat_len = comp_lengths.reshape(-1).astype(jnp.float32)
    length = lax.optimization_barrier(jnp.sum(jnp.where(onehot, flat_len[None, :], 0.0), axis=1)) + (comp_ids == 0).astype(jnp.float32)
    return jnp.where(comp_ids > 0, 64.0 / length, 0.0)

def reference(q_nope, q_rope, latent, latent_gain, k_rope_t, w_uk, w_uv, d_out, group_ids, comp_ids, comp_lengths):
    scaling = 1.0 / math.sqrt(D_NOPE + D_ROPE)
    latent_f = latent.astype(jnp.float32)
    gain_f = latent_gain.astype(jnp.float32)
    inverse = lax.rsqrt(lax.optimization_barrier(jnp.mean(latent_f * latent_f, axis=1, keepdims=True)) + 1e-06)
    normed = (latent_f * inverse * gain_f).astype(jnp.bfloat16)
    position = jnp.arange(TOKENS, dtype=jnp.int32)
    visible = (group_ids[:, None] == group_ids[None, :]) & ((comp_ids[None, :] == 0) | (comp_ids[None, :] == comp_ids[:, None])) & (position[None, :] <= position[:, None])
    weight = token_weights(group_ids, comp_ids, comp_lengths)

    def one_head(running, head_index):
        d_normed, d_rope = running
        query_n = lax.dynamic_slice_in_dim(q_nope, head_index * D_NOPE, D_NOPE, 1)
        query_r = lax.dynamic_slice_in_dim(q_rope, head_index * D_ROPE, D_ROPE, 1)
        key_up = lax.dynamic_slice_in_dim(w_uk, head_index * D_NOPE, D_NOPE, 0)
        value_up = lax.dynamic_slice_in_dim(w_uv, head_index * D_V, D_V, 0)
        grad_out = lax.dynamic_slice_in_dim(d_out, head_index * D_V, D_V, 1)
        q_lat = jnp.dot(query_n, key_up, preferred_element_type=jnp.float32).astype(jnp.bfloat16)
        scores = (jnp.dot(q_lat, normed.T, preferred_element_type=jnp.float32) + jnp.dot(query_r, k_rope_t, preferred_element_type=jnp.float32)) * scaling
        maxima = lax.optimization_barrier(jnp.max(jnp.where(visible, scores, -jnp.inf), axis=1, keepdims=True))
        expos = jnp.where(visible, jnp.exp(scores - maxima), 0.0)
        attention = (expos / lax.optimization_barrier(jnp.sum(expos, axis=1, keepdims=True))).astype(jnp.bfloat16)
        o_lat = jnp.dot(attention, normed, preferred_element_type=jnp.float32).astype(jnp.bfloat16)
        head_out = jnp.dot(o_lat, value_up.T, preferred_element_type=jnp.float32).astype(jnp.bfloat16)
        weighted = (grad_out.astype(jnp.float32) * weight[:, None]).astype(jnp.bfloat16)
        do_lat = jnp.dot(weighted, value_up, preferred_element_type=jnp.float32).astype(jnp.bfloat16)
        grad_wv = jnp.dot(weighted.T, o_lat, preferred_element_type=jnp.float32)
        dprobs = jnp.dot(do_lat, normed.T, preferred_element_type=jnp.float32)
        att_f = attention.astype(jnp.float32)
        row_dot = lax.optimization_barrier(jnp.sum(att_f * dprobs, axis=1, keepdims=True))
        dscores = (att_f * (dprobs - row_dot) * scaling).astype(jnp.bfloat16)
        dq_lat = jnp.dot(dscores, normed, preferred_element_type=jnp.float32).astype(jnp.bfloat16)
        grad_qn = jnp.dot(dq_lat, key_up.T, preferred_element_type=jnp.float32).astype(jnp.bfloat16)
        grad_wk = jnp.dot(query_n.T, dq_lat, preferred_element_type=jnp.float32)
        grad_qr = jnp.dot(dscores, k_rope_t.T, preferred_element_type=jnp.float32).astype(jnp.bfloat16)
        d_normed = d_normed + jnp.dot(dscores.T, q_lat, preferred_element_type=jnp.float32) + jnp.dot(attention.T, do_lat, preferred_element_type=jnp.float32)
        d_rope = d_rope + jnp.dot(query_r.T, dscores, preferred_element_type=jnp.float32)
        return ((d_normed, d_rope), (head_out, grad_qn, grad_qr, grad_wk, grad_wv))
    start_state = (jnp.zeros((TOKENS, D_LAT), jnp.float32), jnp.zeros((D_ROPE, TOKENS), jnp.float32))
    (d_normed, d_rope), stacked = lax.scan(one_head, start_state, jnp.arange(H, dtype=jnp.int32))
    head_out, grad_qn, grad_qr, grad_wk, grad_wv = stacked
    attn_out = jnp.transpose(head_out, (1, 0, 2)).reshape(TOKENS, H * D_V)
    d_q_nope = jnp.transpose(grad_qn, (1, 0, 2)).reshape(TOKENS, H * D_NOPE)
    d_q_rope = jnp.transpose(grad_qr, (1, 0, 2)).reshape(TOKENS, H * D_ROPE)
    lifted = d_normed * gain_f
    d_latent = (inverse * lifted - latent_f * inverse ** 3 * lax.optimization_barrier(jnp.mean(lifted * latent_f, axis=1, keepdims=True))).astype(jnp.bfloat16)
    d_w_uk = grad_wk.reshape(H * D_NOPE, D_LAT).astype(jnp.bfloat16)
    d_w_uv = grad_wv.reshape(H * D_V, D_LAT).astype(jnp.bfloat16)
    return (attn_out, d_q_nope, d_q_rope, d_latent, d_rope.astype(jnp.bfloat16), d_w_uk, d_w_uv)
```

```python
import functools
import math

import jax
import jax.numpy as jnp
from jax import lax
from jax.experimental import pallas as pl
from jax.experimental.pallas import tpu as pltpu
from jax.sharding import Mesh
from jax.sharding import PartitionSpec as P

D_LAT = 512
D_ROPE = 64
D_NOPE = 128
D_V = 128
GROUPS = 2
COMP = 8
CODES = GROUPS * (COMP + 1)
TOKENS = 2048
CTX = 8
ROWS = TOKENS // CTX
BLOCK = 16
TILE = 256
MAX_TILES = 6
WIDE = (3,)
PACK = 640
EXTRA = PACK - D_LAT
PAD_COL = PACK - 1
HIDE = -1e30
SCALING = 1.0 / math.sqrt(D_NOPE + D_ROPE)
BF = jnp.bfloat16
F32 = jnp.float32
CTX_AXES = ("xl", "z")
HEAD_AXES = ("xh", "y", "core")
LOCAL = pltpu.VMEM


def dot(a, b):
    return lax.dot_general(a, b, (((1,), (0,)), ((), ())), preferred_element_type=F32)


def dot_nt(a, b):
    return lax.dot_general(a, b, (((1,), (1,)), ((), ())), preferred_element_type=F32)


def attention_kernel(*refs):
    info, own, mine, other, bias, weight, qn, qr, do, wk, wv = refs[:11]
    out, dqn, dqr, dw, kept, sent = refs[11:17]
    keys, acc, kf, vv, s, dp, e, qf, qt, gb, git, wb, wt, wgrad, meta = refs[17:]
    step = pl.program_id(0)

    def key_rows(t):
        return pl.ds(pl.multiple_of(t * TILE, TILE), TILE)

    @pl.when(step == 0)
    def _():
        chunk, core, group, comp = info[0], info[1], info[2], info[3]
        inside, length, len0, len1 = info[4], info[5], info[6], info[7]
        tags = jnp.sum(
            mine[:, D_LAT:].astype(F32) + other[:, D_LAT:].astype(F32), axis=0, keepdims=True
        )
        lane = lax.broadcasted_iota(jnp.int32, tags.shape, 1) - D_ROPE
        start1 = jnp.sum(jnp.where((lane >= 0) & (lane < COMP + 1), tags, 0.0)).astype(jnp.int32)
        begin = chunk * ROWS
        low1 = jnp.where(group == 0, 0, start1)
        high1 = jnp.minimum(jnp.where(group == 0, start1 - len0, TOKENS - len1), begin)
        block1 = low1 // BLOCK
        n1 = jnp.where(high1 > low1, (high1 + BLOCK - 1) // BLOCK - block1, 0)
        prior = jnp.where(comp > 0, length - inside, 0)
        block2 = jnp.maximum((begin - prior) // BLOCK, jnp.where(n1 > 0, block1 + n1, 0))
        count = n1 + jnp.maximum(begin // BLOCK - block2, 0)
        count = jnp.minimum(count, (MAX_TILES - 1) * (TILE // BLOCK))
        tiles = 1 + (count + TILE // BLOCK - 1) // (TILE // BLOCK)
        meta[0], meta[1], meta[2], meta[3], meta[4] = tiles, n1, block1, block2, count
        keys[0:ROWS, :] = own[...]

        def copy_block(index, carry):
            block = jnp.where(index < n1, block1 + index, block2 + index - n1)
            place = (block // 16) * 8 + block % 8
            rows = pl.ds(pl.multiple_of(place * BLOCK, BLOCK), BLOCK)
            from_mine = ((block % 16) // 8 == core).astype(jnp.int32)
            keys[pl.ds(pl.multiple_of(ROWS + index * BLOCK, BLOCK), BLOCK), :] = jnp.where(
                from_mine == 1, mine[rows, :], other[rows, :]
            )
            return carry

        lax.fori_loop(0, count, copy_block, 0)
        filler = (lax.broadcasted_iota(jnp.int32, (BLOCK, PACK), 1) == PAD_COL).astype(F32).astype(BF)

        def pad_block(index, carry):
            keys[pl.ds(pl.multiple_of(ROWS + index * BLOCK, BLOCK), BLOCK), :] = filler
            return carry

        lax.fori_loop(count, (tiles - 1) * (TILE // BLOCK), pad_block, 0)

        def start_acc(t, carry):
            acc[:, key_rows(t)] = jnp.zeros((acc.shape[0], TILE), F32)
            return carry

        lax.fori_loop(0, tiles, start_acc, 0)

    tiles = meta[0]

    def each_tile(body, carry):
        return lax.fori_loop(0, tiles, body, carry)

    row_weight = weight[...]
    for h in range(2):
        nope = qn[:, h * D_NOPE : (h + 1) * D_NOPE]
        rope = qr[:, h * D_ROPE : (h + 1) * D_ROPE]
        qf[h] = jnp.concatenate([nope, rope, bias[...]], axis=1)
        qt[h] = jnp.concatenate([nope.T, rope.T], axis=0)
        gb[h] = (do[:, h * D_V : (h + 1) * D_V].astype(F32) * row_weight).astype(BF)
        w_head = jnp.concatenate(
            [wk[h * D_NOPE : (h + 1) * D_NOPE, :], wv[h * D_V : (h + 1) * D_V, :]], axis=0
        )
        wb[h * 256 : (h + 1) * 256, :] = w_head
        wt[:, h * 256 : (h + 1) * 256] = w_head.T

    base2 = SCALING * math.log2(math.e)

    def finish_heads(dq, grad):
        for h in range(2):
            dqn[:, h * D_NOPE : (h + 1) * D_NOPE] = dq[h][:, :D_NOPE].astype(BF)
            dw[0, h * D_NOPE : (h + 1) * D_NOPE] = grad[h * 256 : h * 256 + 128].astype(BF)
            dw[1, h * D_V : (h + 1) * D_V] = grad[h * 256 + 128 : (h + 1) * 256].astype(BF)
        dqr[...] = jnp.concatenate(
            [dq[h][:, D_NOPE : D_NOPE + D_ROPE] for h in range(2)], axis=1
        ).astype(BF)

    def wide_step(count):
        width = count * TILE
        all_keys = keys[:width, :]
        both = dot_nt(all_keys[:, :D_LAT], wb[...]).astype(BF)
        shown = lax.broadcasted_iota(jnp.int32, (ROWS, TILE), 1) <= lax.broadcasted_iota(
            jnp.int32, (ROWS, TILE), 0
        )
        parts, rope_sum, dq = [], None, []
        for h in range(2):
            k_full = jnp.concatenate(
                [both[:, h * 256 : h * 256 + 128], all_keys[:, D_LAT:]], axis=1
            )
            value = both[:, h * 256 + 128 : (h + 1) * 256]
            score = dot_nt(qf[h], k_full)
            score = jnp.concatenate(
                [jnp.where(shown, score[:, :TILE], HIDE), score[:, TILE:]], axis=1
            )
            shift = jnp.max(score, axis=1, keepdims=True) * base2
            expo = jnp.exp2(score * base2 - shift)
            inv = 1.0 / jnp.sum(expo, axis=1, keepdims=True)
            expo = expo.astype(BF)
            mixed = dot(expo, value) * inv
            out[:, h * D_V : (h + 1) * D_V] = mixed.astype(BF)
            g = gb[h].astype(F32)
            row_dot = jnp.sum(mixed * g, axis=1, keepdims=True)
            slope = inv * SCALING
            offset = row_dot * slope
            dprobs = dot_nt(gb[h], value)
            ds = (expo.astype(F32) * (dprobs * slope - offset)).astype(BF)
            dq.append(dot(ds, k_full))
            dk = dot(qt[h], ds)
            dv = dot((g * inv).astype(BF).T, expo)
            parts += [dk[:D_NOPE].astype(BF), dv.astype(BF)]
            rope_sum = dk[D_NOPE:] if h == 0 else rope_sum + dk[D_NOPE:]
        dkv = jnp.concatenate(parts, axis=0)
        acc[:D_LAT, :width] += dot(wt[...], dkv)
        acc[D_LAT:, :width] += rope_sum
        finish_heads(dq, dot(dkv, all_keys[:, :D_LAT]))

    def loop_step():
        row = lax.broadcasted_iota(jnp.int32, (ROWS, TILE), 0)
        col = lax.broadcasted_iota(jnp.int32, (ROWS, TILE), 1)

        def score_tile(t, maxima):
            tile_keys = keys[key_rows(t), :]
            both = dot_nt(tile_keys[:, :D_LAT], wb[...]).astype(BF)
            shown = col <= row + t * (MAX_TILES * TILE)
            new = []
            for h in range(2):
                k_nope = both[:, h * 256 : h * 256 + 128]
                value = both[:, h * 256 + 128 : (h + 1) * 256]
                k_full = jnp.concatenate([k_nope, tile_keys[:, D_LAT:]], axis=1)
                kf[h, t] = k_full
                vv[h, t] = value
                score = jnp.where(shown, dot_nt(qf[h], k_full), HIDE)
                s[h, t] = score
                dp[h, t] = dot_nt(gb[h], value)
                new.append(jnp.maximum(maxima[h], jnp.maximum(score[:, :128], score[:, 128:])))
            return tuple(new)

        low = jnp.full((ROWS, 128), HIDE, F32)
        maxima = each_tile(score_tile, (low, low))
        shifts = [jnp.max(m, axis=1, keepdims=True) * base2 for m in maxima]

        def prob_tile(t, carry):
            new = []
            for h in range(2):
                total, mixed = carry[h]
                expo = jnp.exp2(s[h, t] * base2 - shifts[h])
                total = total + (expo[:, :128] + expo[:, 128:])
                expo = expo.astype(BF)
                e[h, t] = expo
                new.append((total, mixed + dot(expo, vv[h, t])))
            return tuple(new)

        nothing = jnp.zeros((ROWS, 128), F32)
        mixes = each_tile(prob_tile, ((nothing, nothing), (nothing, nothing)))
        slopes, offsets = [], []
        for h in range(2):
            total, mixed = mixes[h]
            inv = 1.0 / jnp.sum(total, axis=1, keepdims=True)
            mixed = mixed * inv
            out[:, h * D_V : (h + 1) * D_V] = mixed.astype(BF)
            g = gb[h].astype(F32)
            row_dot = jnp.sum(mixed * g, axis=1, keepdims=True)
            slopes.append(inv * SCALING)
            offsets.append(row_dot * (inv * SCALING))
            git[h] = (g * inv).astype(BF).T

        wgrad[...] = jnp.zeros(wgrad.shape, F32)

        def back_tile(t, carry):
            tile_keys = keys[key_rows(t), :D_LAT]
            parts, rope_sum, new = [], None, []
            for h in range(2):
                expo = e[h, t]
                ds = (expo.astype(F32) * (dp[h, t] * slopes[h] - offsets[h])).astype(BF)
                new.append(carry[h] + dot(ds, kf[h, t]))
                dk = dot(qt[h], ds)
                dv = dot(git[h], expo)
                parts += [dk[:D_NOPE].astype(BF), dv.astype(BF)]
                rope_sum = dk[D_NOPE:] if h == 0 else rope_sum + dk[D_NOPE:]
            dkv = jnp.concatenate(parts, axis=0)
            acc[:D_LAT, key_rows(t)] += dot(wt[...], dkv)
            acc[D_LAT:, key_rows(t)] += rope_sum
            wgrad[...] += dot(dkv, tile_keys)
            return tuple(new)

        empty = jnp.zeros((ROWS, 256), F32)
        dq = each_tile(back_tile, (empty, empty))
        finish_heads(dq, wgrad[...])

    for count in WIDE:

        @pl.when(tiles == count)
        def _(count=count):
            wide_step(count)

    @pl.when(functools.reduce(lambda x, y: x & y, [tiles != count for count in WIDE]))
    def _():
        loop_step()

    @pl.when(step == pl.num_programs(0) - 1)
    def _():
        chunk, core = info[0], info[1]
        n1, block1, block2, count = meta[1], meta[2], meta[3], meta[4]
        kept[...] = jnp.zeros(kept.shape, BF)
        sent[...] = jnp.zeros(sent.shape, BF)

        def turn(t, carry):
            keys[key_rows(t), :D_LAT] = acc[:D_LAT, key_rows(t)].astype(BF).T
            keys[key_rows(t), D_LAT:] = jnp.concatenate(
                [acc[D_LAT:, key_rows(t)].astype(BF), jnp.zeros((EXTRA - D_ROPE, TILE), BF)], axis=0
            ).T
            return carry

        lax.fori_loop(0, tiles, turn, 0)

        def place(index, carry):
            past = index - ROWS // BLOCK
            block = jnp.where(past < n1, block1 + past, block2 + past - n1)
            block = jnp.where(past < 0, chunk * (ROWS // BLOCK) + index, block)
            pair = block // 2
            where = (pair % 4) * 16 + ((pair // 8) % 4) * 4 + (pair // 32) * 2 + (pair // 4) % 2
            rows = pl.ds(pl.multiple_of(where * BLOCK, BLOCK), BLOCK)
            values = keys[pl.ds(pl.multiple_of(index * BLOCK, BLOCK), BLOCK), :]

            @pl.when((block + core) % 2 == 0)
            def _():
                kept[rows, :] = values

            @pl.when((block + core) % 2 == 1)
            def _():
                sent[rows, :] = values

            return carry

        lax.fori_loop(0, ROWS // BLOCK + count, place, 0)


def attention(shared, q_nope, q_rope, d_out, w_uk, w_uv):
    rows = q_nope.shape[0]
    pairs = w_uk.shape[0] // (2 * D_NOPE)

    def columns(size):
        return pl.BlockSpec((rows, size), lambda i: (0, i))

    def heads(size):
        return pl.BlockSpec((size, D_LAT), lambda i: (i, 0))

    whole = pl.BlockSpec(memory_space=pltpu.VMEM)
    in_specs = [pl.BlockSpec(memory_space=pltpu.SMEM)] + [whole] * 5
    in_specs += [columns(256), columns(128), columns(256), heads(256), heads(256)]
    half = jax.ShapeDtypeStruct((TOKENS // 2, PACK), BF)
    return pl.pallas_call(
        attention_kernel,
        grid=(pairs,),
        in_specs=in_specs,
        out_specs=[
            columns(256),
            columns(256),
            columns(128),
            pl.BlockSpec((2, 256, D_LAT), lambda i: (0, i, 0)),
            whole,
            whole,
        ],
        out_shape=[
            jax.ShapeDtypeStruct(q_nope.shape, BF),
            jax.ShapeDtypeStruct(q_nope.shape, BF),
            jax.ShapeDtypeStruct(q_rope.shape, BF),
            jax.ShapeDtypeStruct((2, pairs * 256, D_LAT), BF),
            half,
            half,
        ],
        scratch_shapes=[
            pltpu.VMEM((MAX_TILES * TILE, PACK), BF),
            pltpu.VMEM((D_LAT + D_ROPE, MAX_TILES * TILE), F32),
            pltpu.VMEM((2, MAX_TILES, TILE, 256), BF),
            pltpu.VMEM((2, MAX_TILES, TILE, D_V), BF),
            pltpu.VMEM((2, MAX_TILES, ROWS, TILE), F32),
            pltpu.VMEM((2, MAX_TILES, ROWS, TILE), F32),
            pltpu.VMEM((2, MAX_TILES, ROWS, TILE), BF),
            pltpu.VMEM((2, ROWS, 256), BF),
            pltpu.VMEM((2, D_NOPE + D_ROPE, ROWS), BF),
            pltpu.VMEM((2, ROWS, D_V), BF),
            pltpu.VMEM((2, D_V, ROWS), BF),
            pltpu.VMEM((512, D_LAT), BF),
            pltpu.VMEM((D_LAT, 512), BF),
            pltpu.VMEM((512, D_LAT), F32),
            pltpu.SMEM((8,), jnp.int32),
        ],
        compiler_params=pltpu.CompilerParams(vmem_limit_bytes=56 << 20),
        cost_estimate=pl.CostEstimate(
            flops=pairs * 2600000000, bytes_accessed=16 << 20, transcendentals=pairs * 400000
        ),
        name="attention",
    )(*shared, q_nope, q_rope, d_out, w_uk, w_uv)


def prepare_kernel(latent, gain, rope_t, gid, cid, gid_s, cid_s, lengths, own, send, bias, weight, inverse, info):
    chunk = lax.axis_index("xl") * 4 + lax.axis_index("z")
    core = lax.axis_index("core")
    latent_f = latent[...].astype(F32)
    inv = lax.rsqrt(jnp.mean(latent_f * latent_f, axis=1, keepdims=True) + 1e-06)
    inverse[...] = inv
    normed = (latent_f * inv * gain[...].astype(F32)).astype(BF)
    group = jnp.broadcast_to(gid[...].astype(F32), (8, ROWS)).T[:, :1].astype(jnp.int32)
    comp = jnp.broadcast_to(cid[...].astype(F32), (8, ROWS)).T[:, :1].astype(jnp.int32)
    code = group * (COMP + 1) + comp
    column = lax.broadcasted_iota(jnp.int32, (ROWS, EXTRA - D_ROPE), 1)
    tags = jnp.where(column == code, 1.0, 0.0).astype(BF)
    seen = (column == code) | (column == group * (COMP + 1))
    bias[...] = jnp.where(seen, 0.0, HIDE).astype(BF)
    own[...] = jnp.concatenate([normed, rope_t[...].T, tags], axis=1)
    half = own[pl.ds(pl.multiple_of(core * (ROWS // 2), ROWS // 2), ROWS // 2), :]
    for i in range(CTX):
        send[i] = half
    length = jnp.ones((ROWS, 1), F32)
    for g in range(GROUPS):
        for k in range(COMP):
            length = jnp.where(code == g * (COMP + 1) + k + 1, lengths[g, k].astype(F32), length)
    weight[...] = jnp.where(comp > 0, 64.0 / length, 0.0)
    group0, comp0 = gid_s[0], cid_s[0]
    info[0], info[1], info[2], info[3] = chunk, core, group0, comp0
    info[4] = jnp.sum(
        jnp.where(gid[...] * (COMP + 1) + cid[...] == group0 * (COMP + 1) + comp0, 1.0, 0.0)
    ).astype(jnp.int32)
    info[5] = lengths[group0, jnp.maximum(comp0 - 1, 0)]
    for g in range(GROUPS):
        info[6 + g] = sum([lengths[g, k] for k in range(1, COMP)], lengths[g, 0])


def prepare(latent, latent_gain, k_rope_t, group_ids, comp_ids, comp_lengths):
    vector = pl.BlockSpec(memory_space=LOCAL)
    scalar = pl.BlockSpec(memory_space=pltpu.SMEM)
    return pl.pallas_call(
        prepare_kernel,
        in_specs=[vector] * 5 + [scalar] * 3,
        out_specs=[vector] * 5 + [scalar],
        out_shape=[
            jax.ShapeDtypeStruct((ROWS, PACK), BF),
            jax.ShapeDtypeStruct((CTX, ROWS // 2, PACK), BF),
            jax.ShapeDtypeStruct((ROWS, EXTRA - D_ROPE), BF),
            jax.ShapeDtypeStruct((ROWS, 1), F32),
            jax.ShapeDtypeStruct((ROWS, 1), F32),
            jax.ShapeDtypeStruct((8,), jnp.int32),
        ],
        name="prepare",
    )(
        latent,
        latent_gain[None, :],
        k_rope_t,
        group_ids[None, :],
        comp_ids[None, :],
        group_ids,
        comp_ids,
        comp_lengths,
    )


def relative(axis, distance):
    if axis == "x":
        return (lax.axis_index("xl") * 2 + lax.axis_index("xh")) ^ distance
    return (lax.axis_index(axis) + distance) & 3


def move(x, axis, distance):
    if axis == "x":
        names = ("xl", "xh")
        return lax.ppermute(x, names, [(i, i ^ distance) for i in range(4)])
    return lax.ppermute(x, axis, [(i, (i + distance) % 4) for i in range(4)])


def fold_kernel(axis, count, *refs):
    parts, outs = refs[:count], refs[count:]
    size = outs[0].shape[0]
    for distance in range(4):
        start = pl.multiple_of(relative(axis, distance) * size, BLOCK)
        total = parts[0][pl.ds(start, size), :].astype(F32)
        for part in parts[1:]:
            total = total + part[pl.ds(start, size), :].astype(F32)
        outs[distance][...] = total.astype(BF)


def fold(axis, parts):
    vector = pl.BlockSpec(memory_space=LOCAL)
    shape = jax.ShapeDtypeStruct((parts[0].shape[0] // 4, PACK), BF)
    return pl.pallas_call(
        functools.partial(fold_kernel, axis, len(parts)),
        in_specs=[vector] * len(parts),
        out_specs=[vector] * 4,
        out_shape=[shape] * 4,
        name="fold_" + axis,
    )(*parts)


def scatter(axis, parts):
    cut = fold(axis, parts)
    return [cut[0]] + [move(cut[d], axis, d) for d in (2, 1, 3)]


def finish_kernel(a, b, c, d, latent, inverse, gain, out):
    head = lax.axis_index("xh") * 8 + lax.axis_index("y") * 2 + lax.axis_index("core")
    rows = pl.ds(pl.multiple_of(head * BLOCK, BLOCK), BLOCK)
    total = a[...].astype(F32) + b[...].astype(F32) + c[...].astype(F32) + d[...].astype(F32)
    lifted = total[:, :D_LAT] * gain[...].astype(F32)
    own, inv = latent[rows, :].astype(F32), inverse[rows, :]
    centred = jnp.mean(lifted * own, axis=1, keepdims=True)
    out[:, :D_LAT] = (inv * lifted - own * inv**3 * centred).astype(BF)
    out[:, D_LAT:] = total[:, D_LAT:].astype(BF)


def finish(parts, latent, inverse, latent_gain):
    vector = pl.BlockSpec(memory_space=LOCAL)
    return pl.pallas_call(
        finish_kernel,
        in_specs=[vector] * 7,
        out_specs=vector,
        out_shape=jax.ShapeDtypeStruct((BLOCK, PACK), BF),
        name="finish",
    )(*parts, latent, inverse, latent_gain[None, :])


def assemble_kernel(*refs):
    pieces, out, rope = refs[:16], refs[16], refs[17]
    xh, y, core = lax.axis_index("xh"), lax.axis_index("y"), lax.axis_index("core")
    everything = []
    for index, piece in enumerate(pieces):
        other, place = index // 8, index % 8
        head = (xh ^ (place // 4)) * 8 + ((y - place % 4) & 3) * 2 + (core ^ other)
        rows = pl.ds(pl.multiple_of(head * BLOCK, BLOCK), BLOCK)
        out[rows, :] = piece[:, :D_LAT]
        refs[18][rows, :] = piece[:, D_LAT:].astype(F32)
    rope[...] = refs[18][...].T[:D_ROPE].astype(BF)


def assemble(pieces):
    vector = pl.BlockSpec(memory_space=LOCAL)
    return pl.pallas_call(
        assemble_kernel,
        in_specs=[vector] * 16,
        out_specs=[vector] * 2,
        out_shape=[
            jax.ShapeDtypeStruct((ROWS, D_LAT), BF),
            jax.ShapeDtypeStruct((D_ROPE, ROWS), BF),
        ],
        scratch_shapes=[pltpu.VMEM((ROWS, EXTRA), F32)],
        name="assemble",
    )(*pieces)


def total_kernel(pieces, out):
    total = pieces[0].astype(F32)
    for i in range(1, CTX):
        total = total + pieces[i].astype(F32)
    total = total.astype(BF)
    for i in range(CTX):
        out[i] = total


def total_and_copy(pieces):
    count, rows, width = pieces.shape
    spec = pl.BlockSpec((count, rows // 4, width), lambda i: (0, i, 0))
    return pl.pallas_call(
        total_kernel,
        grid=(4,),
        in_specs=[spec],
        out_specs=spec,
        out_shape=jax.ShapeDtypeStruct(pieces.shape, BF),
        name="total",
    )(pieces)


def swap_core(x):
    return lax.ppermute(x, "core", [(0, 1), (1, 0)])


def exchange(x, axes):
    return lax.all_to_all(x, axes, 0, 0, tiled=True)


def on_device(
    q_nope,
    q_rope,
    latent,
    latent_gain,
    k_rope_t,
    w_uk,
    w_uv,
    d_out,
    group_ids,
    comp_ids,
    comp_lengths,
):
    own, send, bias, weight, inverse, info = prepare(
        latent, latent_gain, k_rope_t, group_ids, comp_ids, comp_lengths
    )
    mine = exchange(send, CTX_AXES).reshape(-1, PACK)
    other = swap_core(mine)
    shared = (info, own, mine, other, bias, weight)
    out, dqn, dqr, dw, kept, sent = attention(shared, q_nope, q_rope, d_out, w_uk, w_uv)
    pieces = exchange(dw.reshape(CTX, -1, D_LAT), CTX_AXES)
    total = total_and_copy(pieces)
    parts = scatter("y", [kept, swap_core(sent)])
    parts, total = lax.optimization_barrier((parts, total))
    weights = exchange(total, CTX_AXES).reshape(2, -1, D_LAT)
    parts = scatter("x", scatter("z", parts))
    final = finish(parts, latent, inverse, latent_gain)
    pieces = [final] + [
        lax.ppermute(
            final,
            ("xh", "y"),
            [(i, ((i // 4) ^ (d // 4)) * 4 + (i + d) % 4) for i in range(8)],
        )
        for d in range(1, 8)
    ]
    swapped = swap_core(jnp.stack(pieces))
    d_latent, d_k_rope_t = assemble(pieces + [swapped[i] for i in range(8)])
    return out, dqn, dqr, d_latent, d_k_rope_t, weights[0], weights[1]


def solution(mesh):
    fine = Mesh(mesh.devices.reshape(2, 4, 2, 4, 2), CTX_AXES + HEAD_AXES)
    return jax.shard_map(
        on_device,
        mesh=fine,
        in_specs=(
            P(CTX_AXES, HEAD_AXES),
            P(CTX_AXES, HEAD_AXES),
            P(CTX_AXES, None),
            P(),
            P(None, CTX_AXES),
            P(HEAD_AXES, None),
            P(HEAD_AXES, None),
            P(CTX_AXES, HEAD_AXES),
            P(CTX_AXES),
            P(CTX_AXES),
            P(),
        ),
        out_specs=(
            P(CTX_AXES, HEAD_AXES),
            P(CTX_AXES, HEAD_AXES),
            P(CTX_AXES, HEAD_AXES),
            P(CTX_AXES, None),
            P(None, CTX_AXES),
            P(HEAD_AXES, None),
            P(HEAD_AXES, None),
        ),
        check_vma=False,
    )
```

```python
import functools
import math

import jax
import jax.numpy as jnp
from jax import lax
from jax.experimental import pallas as pl
from jax.experimental.pallas import tpu as pltpu
from jax.sharding import Mesh
from jax.sharding import PartitionSpec as P

D_LAT = 512
D_ROPE = 64
D_NOPE = 128
D_V = 128
GROUPS = 2
COMP = 8
CODES = GROUPS * (COMP + 1)
TOKENS = 2048
CTX = 8
ROWS = TOKENS // CTX
BLOCK = 16
TILE = 256
MAX_TILES = 6
SLOTS = 12
WIDE = (3, 4)
SMALL = pl.CostEstimate(flops=1, bytes_accessed=1, transcendentals=0)
PACK = 640
EXTRA = PACK - D_LAT
PAD_COL = PACK - 1
HIDE = -1e30
SCALING = 1.0 / math.sqrt(D_NOPE + D_ROPE)
BF = jnp.bfloat16
F32 = jnp.float32
CTX_AXES = ("xl", "z")
HEAD_AXES = ("xh", "y", "core")
LOCAL = pltpu.VMEM


def dot(a, b):
    return lax.dot_general(a, b, (((1,), (0,)), ((), ())), preferred_element_type=F32)


def dot_nt(a, b):
    return lax.dot_general(a, b, (((1,), (1,)), ((), ())), preferred_element_type=F32)


def attention_kernel(*refs):
    info, own, mine, other, bias, weight, qn, qr, do, wk, wv = refs[:11]
    out, dqn, dqr, dw, kept, sent, meta = refs[11:18]
    keys, acc, kf, vv, s, dp, e, qf, qt, gb, git, wb, wt, wgrad = refs[18:]
    step = pl.program_id(0)

    def key_rows(t):
        return pl.ds(pl.multiple_of(t * TILE, TILE), TILE)

    @pl.when(step == 0)
    def _():
        chunk, core, group, comp = info[0], info[1], info[2], info[3]
        inside, length, len0, len1 = info[4], info[5], info[6], info[7]
        tags = jnp.sum(
            mine[:, D_LAT:].astype(F32) + other[:, D_LAT:].astype(F32), axis=0, keepdims=True
        )
        lane = lax.broadcasted_iota(jnp.int32, tags.shape, 1) - D_ROPE
        start1 = jnp.sum(jnp.where((lane >= 0) & (lane < COMP + 1), tags, 0.0)).astype(jnp.int32)
        begin = chunk * ROWS
        low1 = jnp.where(group == 0, 0, start1)
        high1 = jnp.minimum(jnp.where(group == 0, start1 - len0, TOKENS - len1), begin)
        block1 = low1 // BLOCK
        n1 = jnp.where(high1 > low1, (high1 + BLOCK - 1) // BLOCK - block1, 0)
        prior = jnp.where(comp > 0, length - inside, 0)
        block2 = jnp.maximum((begin - prior) // BLOCK, jnp.where(n1 > 0, block1 + n1, 0))
        count = n1 + jnp.maximum(begin // BLOCK - block2, 0)
        count = jnp.minimum(count, (MAX_TILES - 1) * (TILE // BLOCK))
        tiles = 1 + (count + TILE // BLOCK - 1) // (TILE // BLOCK)
        meta[0], meta[1], meta[2], meta[3], meta[4] = tiles, n1, block1, block2, count
        meta[5] = chunk
        keys[0:ROWS, :] = own[...]

        def copy_block(index, carry):
            block = jnp.where(index < n1, block1 + index, block2 + index - n1)
            place = (block // 16) * 8 + block % 8
            rows = pl.ds(pl.multiple_of(place * BLOCK, BLOCK), BLOCK)
            from_mine = ((block % 16) // 8 == core).astype(jnp.int32)
            keys[pl.ds(pl.multiple_of(ROWS + index * BLOCK, BLOCK), BLOCK), :] = jnp.where(
                from_mine == 1, mine[rows, :], other[rows, :]
            )
            return carry

        lax.fori_loop(0, count, copy_block, 0)
        filler = (lax.broadcasted_iota(jnp.int32, (BLOCK, PACK), 1) == PAD_COL).astype(F32).astype(BF)

        def pad_block(index, carry):
            keys[pl.ds(pl.multiple_of(ROWS + index * BLOCK, BLOCK), BLOCK), :] = filler
            return carry

        lax.fori_loop(count, (tiles - 1) * (TILE // BLOCK), pad_block, 0)

        def start_acc(t, carry):
            acc[:, key_rows(t)] = jnp.zeros((acc.shape[0], TILE), F32)
            return carry

        lax.fori_loop(0, tiles, start_acc, 0)

    tiles = meta[0]

    def each_tile(body, carry):
        return lax.fori_loop(0, tiles, body, carry)

    row_weight = weight[...]
    for h in range(2):
        nope = qn[:, h * D_NOPE : (h + 1) * D_NOPE]
        rope = qr[:, h * D_ROPE : (h + 1) * D_ROPE]
        qf[h] = jnp.concatenate([nope, rope, bias[...]], axis=1)
        qt[h] = jnp.concatenate([nope.T, rope.T], axis=0)
        gb[h] = (do[:, h * D_V : (h + 1) * D_V].astype(F32) * row_weight).astype(BF)
        w_head = jnp.concatenate(
            [wk[h * D_NOPE : (h + 1) * D_NOPE, :], wv[h * D_V : (h + 1) * D_V, :]], axis=0
        )
        wb[h * 256 : (h + 1) * 256, :] = w_head
        wt[:, h * 256 : (h + 1) * 256] = w_head.T

    base2 = SCALING * math.log2(math.e)

    def add_grads(cols, lat_grads, rope_grads):
        acc[:D_LAT, cols] += lat_grads
        acc[D_LAT:, cols] += rope_grads

    def finish_heads(dq, grad):
        for h in range(2):
            dqn[:, h * D_NOPE : (h + 1) * D_NOPE] = dq[h][:, :D_NOPE].astype(BF)
            dw[h] = grad[h * 256 : (h + 1) * 256].astype(BF)
        dqr[...] = jnp.concatenate(
            [dq[h][:, D_NOPE : D_NOPE + D_ROPE] for h in range(2)], axis=1
        ).astype(BF)

    def wide_step(count):
        width = count * TILE
        all_keys = keys[:width, :]
        both = dot_nt(all_keys[:, :D_LAT], wb[...]).astype(BF)
        shown = lax.broadcasted_iota(jnp.int32, (ROWS, TILE), 1) <= lax.broadcasted_iota(
            jnp.int32, (ROWS, TILE), 0
        )
        parts, rope_sum, dq = [], None, []
        for h in range(2):
            k_full = jnp.concatenate(
                [both[:, h * 256 : h * 256 + 128], all_keys[:, D_LAT:]], axis=1
            )
            value = both[:, h * 256 + 128 : (h + 1) * 256]
            score = dot_nt(qf[h], k_full)
            score = jnp.concatenate(
                [jnp.where(shown, score[:, :TILE], HIDE), score[:, TILE:]], axis=1
            )
            shift = jnp.max(score, axis=1, keepdims=True) * base2
            expo = jnp.exp2(score * base2 - shift)
            inv = 1.0 / jnp.sum(expo, axis=1, keepdims=True)
            expo = expo.astype(BF)
            mixed = dot(expo, value) * inv
            out[:, h * D_V : (h + 1) * D_V] = mixed.astype(BF)
            g = gb[h].astype(F32)
            row_dot = jnp.sum(mixed * g, axis=1, keepdims=True)
            slope = inv * SCALING
            offset = row_dot * slope
            dprobs = dot_nt(gb[h], value)
            ds = (expo.astype(F32) * (dprobs * slope - offset)).astype(BF)
            dq.append(dot(ds, k_full))
            dk = dot(qt[h], ds)
            dv = dot((g * inv).astype(BF).T, expo)
            parts += [dk[:D_NOPE].astype(BF), dv.astype(BF)]
            rope_sum = dk[D_NOPE:] if h == 0 else rope_sum + dk[D_NOPE:]
        dkv = jnp.concatenate(parts, axis=0)
        add_grads(slice(0, width), dot(wt[...], dkv), rope_sum)
        finish_heads(dq, dot(dkv, all_keys[:, :D_LAT]))

    def loop_step():
        row = lax.broadcasted_iota(jnp.int32, (ROWS, TILE), 0)
        col = lax.broadcasted_iota(jnp.int32, (ROWS, TILE), 1)

        def score_tile(t, maxima):
            tile_keys = keys[key_rows(t), :]
            both = dot_nt(tile_keys[:, :D_LAT], wb[...]).astype(BF)
            shown = col <= row + t * (MAX_TILES * TILE)
            new = []
            for h in range(2):
                k_nope = both[:, h * 256 : h * 256 + 128]
                value = both[:, h * 256 + 128 : (h + 1) * 256]
                k_full = jnp.concatenate([k_nope, tile_keys[:, D_LAT:]], axis=1)
                kf[h, t] = k_full
                vv[h, t] = value
                score = jnp.where(shown, dot_nt(qf[h], k_full), HIDE)
                s[h, t] = score
                dp[h, t] = dot_nt(gb[h], value)
                new.append(jnp.maximum(maxima[h], jnp.maximum(score[:, :128], score[:, 128:])))
            return tuple(new)

        low = jnp.full((ROWS, 128), HIDE, F32)
        maxima = each_tile(score_tile, (low, low))
        shifts = [jnp.max(m, axis=1, keepdims=True) * base2 for m in maxima]

        def prob_tile(t, carry):
            new = []
            for h in range(2):
                total, mixed = carry[h]
                expo = jnp.exp2(s[h, t] * base2 - shifts[h])
                total = total + (expo[:, :128] + expo[:, 128:])
                expo = expo.astype(BF)
                e[h, t] = expo
                new.append((total, mixed + dot(expo, vv[h, t])))
            return tuple(new)

        nothing = jnp.zeros((ROWS, 128), F32)
        mixes = each_tile(prob_tile, ((nothing, nothing), (nothing, nothing)))
        slopes, offsets = [], []
        for h in range(2):
            total, mixed = mixes[h]
            inv = 1.0 / jnp.sum(total, axis=1, keepdims=True)
            mixed = mixed * inv
            out[:, h * D_V : (h + 1) * D_V] = mixed.astype(BF)
            g = gb[h].astype(F32)
            row_dot = jnp.sum(mixed * g, axis=1, keepdims=True)
            slopes.append(inv * SCALING)
            offsets.append(row_dot * (inv * SCALING))
            git[h] = (g * inv).astype(BF).T

        wgrad[...] = jnp.zeros(wgrad.shape, F32)

        def back_tile(t, carry):
            tile_keys = keys[key_rows(t), :D_LAT]
            parts, rope_sum, new = [], None, []
            for h in range(2):
                expo = e[h, t]
                ds = (expo.astype(F32) * (dp[h, t] * slopes[h] - offsets[h])).astype(BF)
                new.append(carry[h] + dot(ds, kf[h, t]))
                dk = dot(qt[h], ds)
                dv = dot(git[h], expo)
                parts += [dk[:D_NOPE].astype(BF), dv.astype(BF)]
                rope_sum = dk[D_NOPE:] if h == 0 else rope_sum + dk[D_NOPE:]
            dkv = jnp.concatenate(parts, axis=0)
            add_grads(key_rows(t), dot(wt[...], dkv), rope_sum)
            wgrad[...] += dot(dkv, tile_keys)
            return tuple(new)

        empty = jnp.zeros((ROWS, 256), F32)
        dq = each_tile(back_tile, (empty, empty))
        finish_heads(dq, wgrad[...])

    for count in WIDE:

        @pl.when(tiles == count)
        def _(count=count):
            wide_step(count)

    @pl.when(functools.reduce(lambda x, y: x & y, [tiles != count for count in WIDE]))
    def _():
        loop_step()

    @pl.when(step == pl.num_programs(0) - 1)
    def _():
        chunk, core = info[0], info[1]
        n1, block1, block2, count = meta[1], meta[2], meta[3], meta[4]
        kept[...] = jnp.zeros(kept.shape, BF)
        sent[...] = jnp.zeros(sent.shape, BF)

        def turn(t, carry):
            keys[key_rows(t), :D_LAT] = acc[:D_LAT, key_rows(t)].astype(BF).T
            keys[key_rows(t), D_LAT:] = jnp.concatenate(
                [acc[D_LAT:, key_rows(t)].astype(BF), jnp.zeros((EXTRA - D_ROPE, TILE), BF)], axis=0
            ).T
            return carry

        lax.fori_loop(0, tiles, turn, 0)

        def put(target, slot, y, index):
            target[slot, y] = keys[pl.ds(pl.multiple_of(index * BLOCK, BLOCK), BLOCK), :]

        own_blocks = ROWS // BLOCK
        for y in range(4):
            for target, parity in ((kept, core), (sent, 1 - core)):
                kind = 2 * y + parity
                for i in range(2):
                    put(target, i, y, 8 * i + kind)
                slot = 2
                for start, shift, length in ((block1, 0, n1), (block2, n1, count - n1)):
                    skip = (kind - start) & 7
                    number = jnp.maximum(length - skip + 7, 0) // 8

                    def put_next(i, carry, target=target, y=y, slot=slot, skip=skip, shift=shift):
                        put(target, slot + i, y, own_blocks + shift + skip + 8 * i)
                        return carry

                    lax.fori_loop(0, number, put_next, 0)
                    slot = slot + number


def attention(shared, q_nope, q_rope, d_out, w_uk, w_uv):
    rows = q_nope.shape[0]
    pairs = w_uk.shape[0] // (2 * D_NOPE)

    def columns(size):
        return pl.BlockSpec((rows, size), lambda i: (0, i))

    def heads(size):
        return pl.BlockSpec((size, D_LAT), lambda i: (i, 0))

    whole = pl.BlockSpec(memory_space=pltpu.VMEM)
    in_specs = [pl.BlockSpec(memory_space=pltpu.SMEM)] + [whole] * 5
    in_specs += [columns(256), columns(128), columns(256), heads(256), heads(256)]
    half = jax.ShapeDtypeStruct((SLOTS, 4, BLOCK, PACK), BF)
    return pl.pallas_call(
        attention_kernel,
        grid=(pairs,),
        in_specs=in_specs,
        out_specs=[
            columns(256),
            columns(256),
            columns(128),
            pl.BlockSpec((2, 256, D_LAT), lambda i: (i, 0, 0)),
            whole,
            whole,
            pl.BlockSpec(memory_space=pltpu.SMEM),
        ],
        out_shape=[
            jax.ShapeDtypeStruct(q_nope.shape, BF),
            jax.ShapeDtypeStruct(q_nope.shape, BF),
            jax.ShapeDtypeStruct(q_rope.shape, BF),
            jax.ShapeDtypeStruct((2 * pairs, 256, D_LAT), BF),
            half,
            half,
            jax.ShapeDtypeStruct((8,), jnp.int32),
        ],
        scratch_shapes=[
            pltpu.VMEM((MAX_TILES * TILE, PACK), BF),
            pltpu.VMEM((D_LAT + D_ROPE, MAX_TILES * TILE), F32),
            pltpu.VMEM((2, MAX_TILES, TILE, 256), BF),
            pltpu.VMEM((2, MAX_TILES, TILE, D_V), BF),
            pltpu.VMEM((2, MAX_TILES, ROWS, TILE), F32),
            pltpu.VMEM((2, MAX_TILES, ROWS, TILE), F32),
            pltpu.VMEM((2, MAX_TILES, ROWS, TILE), BF),
            pltpu.VMEM((2, ROWS, 256), BF),
            pltpu.VMEM((2, D_NOPE + D_ROPE, ROWS), BF),
            pltpu.VMEM((2, ROWS, D_V), BF),
            pltpu.VMEM((2, D_V, ROWS), BF),
            pltpu.VMEM((512, D_LAT), BF),
            pltpu.VMEM((D_LAT, 512), BF),
            pltpu.VMEM((512, D_LAT), F32),
        ],
        compiler_params=pltpu.CompilerParams(vmem_limit_bytes=56 << 20),
        cost_estimate=pl.CostEstimate(
            flops=pairs * 2600000000, bytes_accessed=16 << 20, transcendentals=pairs * 400000
        ),
        name="attention",
    )(*shared, q_nope, q_rope, d_out, w_uk, w_uv)


def prepare_kernel(latent, gain, rope_t, gid, cid, gid_s, cid_s, lengths, own, send, bias, weight, inverse, info):
    chunk = lax.axis_index("xl") * 4 + lax.axis_index("z")
    core = lax.axis_index("core")
    latent_f = latent[...].astype(F32)
    inv = lax.rsqrt(jnp.mean(latent_f * latent_f, axis=1, keepdims=True) + 1e-06)
    inverse[...] = inv
    normed = (latent_f * inv * gain[...].astype(F32)[None, :]).astype(BF)
    group = jnp.broadcast_to(gid[...].astype(F32), (8, ROWS)).T[:, :1].astype(jnp.int32)
    comp = jnp.broadcast_to(cid[...].astype(F32), (8, ROWS)).T[:, :1].astype(jnp.int32)
    code = group * (COMP + 1) + comp
    column = lax.broadcasted_iota(jnp.int32, (ROWS, EXTRA - D_ROPE), 1)
    tags = jnp.where(column == code, 1.0, 0.0).astype(BF)
    seen = (column == code) | (column == group * (COMP + 1))
    bias[...] = jnp.where(seen, 0.0, HIDE).astype(BF)
    own[...] = jnp.concatenate([normed, rope_t[...].T, tags], axis=1)
    half = own[pl.ds(pl.multiple_of(core * (ROWS // 2), ROWS // 2), ROWS // 2), :]
    for i in range(CTX):
        send[i] = half
    length = jnp.ones((ROWS, 1), F32)
    for g in range(GROUPS):
        for k in range(COMP):
            length = jnp.where(code == g * (COMP + 1) + k + 1, lengths[g, k].astype(F32), length)
    weight[...] = jnp.where(comp > 0, 64.0 / length, 0.0)
    group0, comp0 = gid_s[0], cid_s[0]
    info[0], info[1], info[2], info[3] = chunk, core, group0, comp0
    info[4] = jnp.sum(
        jnp.where(gid[...] * (COMP + 1) + cid[...] == group0 * (COMP + 1) + comp0, 1.0, 0.0)
    ).astype(jnp.int32)
    info[5] = lengths[group0, jnp.maximum(comp0 - 1, 0)]
    for g in range(GROUPS):
        info[6 + g] = sum([lengths[g, k] for k in range(1, COMP)], lengths[g, 0])


def prepare(latent, latent_gain, k_rope_t, group_ids, comp_ids, comp_lengths):
    vector = pl.BlockSpec(memory_space=LOCAL)
    scalar = pl.BlockSpec(memory_space=pltpu.SMEM)
    return pl.pallas_call(
        prepare_kernel,
        in_specs=[vector] * 5 + [scalar] * 3,
        out_specs=[vector] * 5 + [scalar],
        out_shape=[
            jax.ShapeDtypeStruct((ROWS, PACK), BF),
            jax.ShapeDtypeStruct((CTX, ROWS // 2, PACK), BF),
            jax.ShapeDtypeStruct((ROWS, EXTRA - D_ROPE), BF),
            jax.ShapeDtypeStruct((ROWS, 1), F32),
            jax.ShapeDtypeStruct((ROWS, 1), F32),
            jax.ShapeDtypeStruct((8,), jnp.int32),
        ],
        cost_estimate=SMALL,
        name="prepare",
    )(
        latent,
        latent_gain,
        k_rope_t,
        group_ids[None, :],
        comp_ids[None, :],
        group_ids,
        comp_ids,
        comp_lengths,
    )


def move(x, axis, distance):
    if axis == "x":
        names = ("xl", "xh")
        return lax.ppermute(x, names, [(i, i ^ distance) for i in range(4)])
    return lax.ppermute(x, axis, [(i, (i + distance) % 4) for i in range(4)])


def summed(parts, index):
    total = parts[0][index].astype(F32)
    for part in parts[1:]:
        total = total + part[index].astype(F32)
    return total.astype(BF)


def fold_y_kernel(*refs):
    parts, outs = refs[:2], refs[2:]
    slots = outs[0].shape[0]
    for distance, out in enumerate(outs):
        place = (lax.axis_index("y") + distance) & 3
        for slot in range(slots):
            out[slot] = summed(parts, (slot, place))


def fold_z_kernel(*refs):
    meta, parts, outs = refs[0], refs[1:5], refs[5:9]
    n1, block1, block2, count, chunk = meta[1], meta[2], meta[3], meta[4], meta[5]
    kind = 2 * lax.axis_index("y") + lax.axis_index("core")
    z = lax.axis_index("z")
    spread = refs[9]
    spread[...] = jnp.zeros(spread.shape, BF)

    def put(slot, block):
        pair = block // 8
        spread[(((pair // 2) % 4) - z) & 3, (pair // 8) * 2 + pair % 2] = summed(parts, (slot,))

    for i in range(2):
        put(i, chunk * (ROWS // BLOCK) + 8 * i + kind)
    slot = 2
    for start, length in ((block1, n1), (block2, count - n1)):
        skip = (kind - start) & 7
        number = jnp.maximum(length - skip + 7, 0) // 8

        def put_next(i, carry, slot=slot, first=start + skip):
            put(slot + i, first + 8 * i)
            return carry

        lax.fori_loop(0, number, put_next, 0)
        slot = slot + number
    for distance, out in enumerate(outs):
        out[...] = spread[distance]


def fold_x_kernel(*refs):
    parts, outs = refs[:4], refs[4:]
    for distance, out in enumerate(outs):
        place = lax.axis_index("xl") ^ distance
        for xh in range(2):
            out[xh] = summed(parts, (place * 2 + xh,))


def fold(kernel, operands, cuts, shape, scratch=()):
    vector = pl.BlockSpec(memory_space=LOCAL)
    scalar = pl.BlockSpec(memory_space=pltpu.SMEM)
    return pl.pallas_call(
        kernel,
        in_specs=[scalar if x.dtype == jnp.int32 else vector for x in operands],
        out_specs=[vector] * cuts,
        out_shape=[jax.ShapeDtypeStruct(shape, BF)] * cuts,
        scratch_shapes=scratch,
        cost_estimate=SMALL,
        name="fold",
    )(*operands)


def gather_grads(kept, sent, meta):
    slots = sent.shape[0]
    cut = fold(fold_y_kernel, [kept, swap_core(sent)], 4, (slots, BLOCK, PACK))
    parts = [cut[0]] + [move(cut[d], "y", d) for d in (2, 1, 3)]
    spread = pltpu.VMEM((4, 4, BLOCK, PACK), BF)
    cut = fold(fold_z_kernel, [meta] + parts, 4, (4, BLOCK, PACK), [spread])
    parts = [cut[0]] + [move(cut[d], "z", d) for d in (2, 1, 3)]
    cut = fold(fold_x_kernel, parts, 2, (2, BLOCK, PACK))
    return [cut[0], move(cut[0], "x", 1), move(cut[1], "x", 2), move(cut[1], "x", 3)]


def finish_kernel(a, b, c, d, latent, inverse, gain, out):
    head = lax.axis_index("y") * 2 + lax.axis_index("core")
    total = sum([part[...].astype(F32) for part in (b, c, d)], a[...].astype(F32))
    total = total.reshape(2 * BLOCK, PACK)
    lifted = total[:, :D_LAT] * gain[...].astype(F32)[None, :]
    places = [pl.ds(pl.multiple_of((xh * 8 + head) * BLOCK, BLOCK), BLOCK) for xh in range(2)]
    own = jnp.concatenate([latent[rows, :] for rows in places], axis=0).astype(F32)
    inv = jnp.concatenate([inverse[rows, :] for rows in places], axis=0)
    centred = jnp.mean(lifted * own, axis=1, keepdims=True)
    out[:, :D_LAT] = (inv * lifted - own * inv**3 * centred).astype(BF)
    out[:, D_LAT:] = total[:, D_LAT:].astype(BF)


def finish(parts, latent, inverse, latent_gain):
    vector = pl.BlockSpec(memory_space=LOCAL)
    return pl.pallas_call(
        finish_kernel,
        in_specs=[vector] * 7,
        out_specs=vector,
        out_shape=jax.ShapeDtypeStruct((2 * BLOCK, PACK), BF),
        cost_estimate=SMALL,
        name="finish",
    )(*parts, latent, inverse, latent_gain)


def assemble_kernel(*refs):
    pieces, out, rope, turned = refs[:4], refs[4], refs[5], refs[6]
    y, core = lax.axis_index("y"), lax.axis_index("core")
    for distance, piece in enumerate(pieces):
        for other in range(2):
            for xh in range(2):
                head = xh * 8 + ((y - distance) & 3) * 2 + (core ^ other)
                rows = pl.ds(pl.multiple_of(head * BLOCK, BLOCK), BLOCK)
                place = (other * 2 + xh) * BLOCK
                out[rows, :] = piece[place : place + BLOCK, :D_LAT]
                turned[rows, :] = piece[place : place + BLOCK, D_LAT:].astype(F32)
    rope[...] = turned[...].T[:D_ROPE].astype(BF)


def assemble(pieces):
    vector = pl.BlockSpec(memory_space=LOCAL)
    return pl.pallas_call(
        assemble_kernel,
        in_specs=[vector] * 4,
        out_specs=[vector] * 2,
        out_shape=[
            jax.ShapeDtypeStruct((ROWS, D_LAT), BF),
            jax.ShapeDtypeStruct((D_ROPE, ROWS), BF),
        ],
        scratch_shapes=[pltpu.VMEM((ROWS, EXTRA), F32)],
        cost_estimate=SMALL,
        name="assemble",
    )(*pieces)


def total_kernel(pieces, out, parts, sums, in_sems, out_sems):
    steps = in_sems.shape[0]
    size = sums.shape[0] // steps

    def load(step):
        rows = pl.ds(step * size, size)
        return pltpu.make_async_copy(pieces.at[:, rows, :], parts.at[:, rows, :], in_sems.at[step])

    def store(step, i):
        rows = pl.ds(step * size, size)
        return pltpu.make_async_copy(sums.at[rows, :], out.at[i, rows, :], out_sems.at[step, i])

    for step in range(steps):
        load(step).start()
    for step in range(steps):
        load(step).wait()
        rows = pl.ds(step * size, size)
        total = parts[0, rows, :].astype(F32)
        for i in range(1, CTX):
            total = total + parts[i, rows, :].astype(F32)
        sums[rows, :] = total.astype(BF)
        for i in range(CTX):
            store(step, i).start()
    for step in range(steps):
        for i in range(CTX):
            store(step, i).wait()


def total_and_copy(pieces):
    anywhere = pl.BlockSpec(memory_space=pl.ANY)
    return pl.pallas_call(
        total_kernel,
        in_specs=[anywhere],
        out_specs=anywhere,
        out_shape=jax.ShapeDtypeStruct(pieces.shape, BF),
        scratch_shapes=[
            pltpu.VMEM(pieces.shape, BF),
            pltpu.VMEM(pieces.shape[1:], BF),
            pltpu.SemaphoreType.DMA((4,)),
            pltpu.SemaphoreType.DMA((4, CTX)),
        ],
        compiler_params=pltpu.CompilerParams(vmem_limit_bytes=56 << 20),
        cost_estimate=SMALL,
        name="total",
    )(pieces)


def swap_core(x):
    return lax.ppermute(x, "core", [(0, 1), (1, 0)])


def exchange(x, axes):
    return lax.all_to_all(x, axes, 0, 0, tiled=True)


def on_device(
    q_nope,
    q_rope,
    latent,
    latent_gain,
    k_rope_t,
    w_uk,
    w_uv,
    d_out,
    group_ids,
    comp_ids,
    comp_lengths,
):
    own, send, bias, weight, inverse, info = prepare(
        latent, latent_gain, k_rope_t, group_ids, comp_ids, comp_lengths
    )
    mine = exchange(send, CTX_AXES).reshape(-1, PACK)
    other = swap_core(mine)
    shared = (info, own, mine, other, bias, weight)
    out, dqn, dqr, dw, kept, sent, meta = attention(shared, q_nope, q_rope, d_out, w_uk, w_uv)
    pieces = exchange(dw, CTX_AXES)
    total = total_and_copy(pieces)
    parts = gather_grads(kept, sent, meta)
    parts, total = lax.optimization_barrier((parts, total))
    weights = exchange(total, CTX_AXES)
    final = finish(parts, latent, inverse, latent_gain)
    pair = jnp.concatenate([final, swap_core(final)], axis=0)
    d_latent, d_k_rope_t = assemble([pair] + [move(pair, "y", d) for d in (1, 2, 3)])
    return out, dqn, dqr, d_latent, d_k_rope_t, *[
        weights[:, i * D_NOPE : (i + 1) * D_NOPE].reshape(-1, D_LAT) for i in range(2)
    ]


def solution(mesh):
    fine = Mesh(mesh.devices.reshape(2, 4, 2, 4, 2), CTX_AXES + HEAD_AXES)
    return jax.shard_map(
        on_device,
        mesh=fine,
        in_specs=(
            P(CTX_AXES, HEAD_AXES),
            P(CTX_AXES, HEAD_AXES),
            P(CTX_AXES, None),
            P(),
            P(None, CTX_AXES),
            P(HEAD_AXES, None),
            P(HEAD_AXES, None),
            P(CTX_AXES, HEAD_AXES),
            P(CTX_AXES),
            P(CTX_AXES),
            P(),
        ),
        out_specs=(
            P(CTX_AXES, HEAD_AXES),
            P(CTX_AXES, HEAD_AXES),
            P(CTX_AXES, HEAD_AXES),
            P(CTX_AXES, None),
            P(None, CTX_AXES),
            P(HEAD_AXES, None),
            P(HEAD_AXES, None),
        ),
        check_vma=False,
    )
```

```python
import functools
import math

import jax
import jax.numpy as jnp
from jax import lax
from jax.experimental import pallas as pl
from jax.experimental.pallas import tpu as pltpu
from jax.sharding import Mesh
from jax.sharding import PartitionSpec as P

D_LAT = 512
D_ROPE = 64
D_NOPE = 128
D_V = 128
GROUPS = 2
COMP = 8
CODES = GROUPS * (COMP + 1)
TOKENS = 2048
CTX = 8
ROWS = TOKENS // CTX
BLOCK = 16
TILE = 256
MAX_TILES = 6
SLOTS = 12
WIDE = (3, 4)
LONG = pl.CostEstimate(flops=100000000000, bytes_accessed=1, transcendentals=0)
SMALL = pl.CostEstimate(flops=1, bytes_accessed=1, transcendentals=0)
PACK = 640
EXTRA = PACK - D_LAT
PAD_COL = PACK - 1
HIDE = -1e30
SCALING = 1.0 / math.sqrt(D_NOPE + D_ROPE)
BF = jnp.bfloat16
F32 = jnp.float32
CTX_AXES = ("xl", "z")
HEAD_AXES = ("xh", "y", "core")
LOCAL = pltpu.VMEM


def dot(a, b):
    return lax.dot_general(a, b, (((1,), (0,)), ((), ())), preferred_element_type=F32)


def dot_nt(a, b):
    return lax.dot_general(a, b, (((1,), (1,)), ((), ())), preferred_element_type=F32)


def attention_kernel(*refs):
    info, own, mine, other, bias, weight, qn, qr, do, wk, wv = refs[:11]
    out, dqn, dqr, dw, kept, sent, meta = refs[11:18]
    keys, acc, kf, vv, s, dp, e, qf, qt, gb, git, wb, wt, wgrad = refs[18:]
    step = pl.program_id(0)

    def key_rows(t):
        return pl.ds(pl.multiple_of(t * TILE, TILE), TILE)

    @pl.when(step == 0)
    def _():
        chunk, core, group, comp = info[0], info[1], info[2], info[3]
        inside, length, len0, len1 = info[4], info[5], info[6], info[7]
        tags = jnp.sum(
            mine[:, D_LAT:].astype(F32) + other[:, D_LAT:].astype(F32), axis=0, keepdims=True
        )
        lane = lax.broadcasted_iota(jnp.int32, tags.shape, 1) - D_ROPE
        start1 = jnp.sum(jnp.where((lane >= 0) & (lane < COMP + 1), tags, 0.0)).astype(jnp.int32)
        begin = chunk * ROWS
        low1 = jnp.where(group == 0, 0, start1)
        high1 = jnp.minimum(jnp.where(group == 0, start1 - len0, TOKENS - len1), begin)
        block1 = low1 // BLOCK
        n1 = jnp.where(high1 > low1, (high1 + BLOCK - 1) // BLOCK - block1, 0)
        prior = jnp.where(comp > 0, length - inside, 0)
        block2 = jnp.maximum((begin - prior) // BLOCK, jnp.where(n1 > 0, block1 + n1, 0))
        count = n1 + jnp.maximum(begin // BLOCK - block2, 0)
        count = jnp.minimum(count, (MAX_TILES - 1) * (TILE // BLOCK))
        tiles = 1 + (count + TILE // BLOCK - 1) // (TILE // BLOCK)
        meta[0], meta[1], meta[2], meta[3], meta[4] = tiles, n1, block1, block2, count
        meta[5] = chunk
        keys[0:ROWS, :] = own[...]

        def copy_block(index, carry):
            block = jnp.where(index < n1, block1 + index, block2 + index - n1)
            place = (block // 16) * 8 + block % 8
            rows = pl.ds(pl.multiple_of(place * BLOCK, BLOCK), BLOCK)
            from_mine = ((block % 16) // 8 == core).astype(jnp.int32)
            keys[pl.ds(pl.multiple_of(ROWS + index * BLOCK, BLOCK), BLOCK), :] = jnp.where(
                from_mine == 1, mine[rows, :], other[rows, :]
            )
            return carry

        lax.fori_loop(0, count, copy_block, 0)
        filler = (lax.broadcasted_iota(jnp.int32, (BLOCK, PACK), 1) == PAD_COL).astype(F32).astype(BF)

        def pad_block(index, carry):
            keys[pl.ds(pl.multiple_of(ROWS + index * BLOCK, BLOCK), BLOCK), :] = filler
            return carry

        lax.fori_loop(count, (tiles - 1) * (TILE // BLOCK), pad_block, 0)

        def start_acc(t, carry):
            acc[:, key_rows(t)] = jnp.zeros((acc.shape[0], TILE), F32)
            return carry

        lax.fori_loop(0, tiles, start_acc, 0)

    tiles = meta[0]

    def each_tile(body, carry):
        return lax.fori_loop(0, tiles, body, carry)

    row_weight = weight[...]
    for h in range(2):
        nope = qn[:, h * D_NOPE : (h + 1) * D_NOPE]
        rope = qr[:, h * D_ROPE : (h + 1) * D_ROPE]
        qf[h] = jnp.concatenate([nope, rope, bias[...]], axis=1)
        qt[h] = jnp.concatenate([nope.T, rope.T], axis=0)
        gb[h] = (do[:, h * D_V : (h + 1) * D_V].astype(F32) * row_weight).astype(BF)
        w_head = jnp.concatenate(
            [wk[h * D_NOPE : (h + 1) * D_NOPE, :], wv[h * D_V : (h + 1) * D_V, :]], axis=0
        )
        wb[h * 256 : (h + 1) * 256, :] = w_head
        wt[:, h * 256 : (h + 1) * 256] = w_head.T

    base2 = SCALING * math.log2(math.e)

    def add_grads(cols, lat_grads, rope_grads):
        acc[:D_LAT, cols] += lat_grads
        acc[D_LAT:, cols] += rope_grads

    def finish_heads(dq, grad):
        for h in range(2):
            dqn[:, h * D_NOPE : (h + 1) * D_NOPE] = dq[h][:, :D_NOPE].astype(BF)
            dw[h] = grad[h * 256 : (h + 1) * 256].astype(BF)
        dqr[...] = jnp.concatenate(
            [dq[h][:, D_NOPE : D_NOPE + D_ROPE] for h in range(2)], axis=1
        ).astype(BF)

    def wide_step(count):
        width = count * TILE
        all_keys = keys[:width, :]
        both = dot_nt(all_keys[:, :D_LAT], wb[...]).astype(BF)
        shown = lax.broadcasted_iota(jnp.int32, (ROWS, TILE), 1) <= lax.broadcasted_iota(
            jnp.int32, (ROWS, TILE), 0
        )
        heads = range(2)
        parts, rope_sum, dq = [], None, []
        k_fulls = [jnp.concatenate([both[:, h * 256 : h * 256 + 128], all_keys[:, D_LAT:]], axis=1) for h in heads]
        values = [both[:, h * 256 + 128 : (h + 1) * 256] for h in heads]
        scores = [dot_nt(qf[h], k_fulls[h]) for h in heads]
        scores = [jnp.concatenate([jnp.where(shown, x[:, :TILE], HIDE), x[:, TILE:]], axis=1) for x in scores]
        dprobs = [dot_nt(gb[h], values[h]) for h in heads]
        expos = [jnp.exp2(x * base2 - jnp.max(x, axis=1, keepdims=True) * base2) for x in scores]
        invs = [1.0 / jnp.sum(x, axis=1, keepdims=True) for x in expos]
        expos = [x.astype(BF) for x in expos]
        mixes = [dot(expos[h], values[h]) * invs[h] for h in heads]
        gs = [gb[h].astype(F32) for h in heads]
        dvs = [dot((gs[h] * invs[h]).astype(BF).T, expos[h]) for h in heads]
        dss = []
        for h in heads:
            out[:, h * D_V : (h + 1) * D_V] = mixes[h].astype(BF)
            slope = invs[h] * SCALING
            offset = jnp.sum(mixes[h] * gs[h], axis=1, keepdims=True) * slope
            dss.append((expos[h].astype(F32) * (dprobs[h] * slope - offset)).astype(BF))
        dks = [dot(qt[h], dss[h]) for h in heads]
        dq = [dot(dss[h], k_fulls[h]) for h in heads]
        for h in heads:
            parts += [dks[h][:D_NOPE].astype(BF), dvs[h].astype(BF)]
        rope_sum = dks[0][D_NOPE:] + dks[1][D_NOPE:]
        dkv = jnp.concatenate(parts, axis=0)
        add_grads(slice(0, width), dot(wt[...], dkv), rope_sum)
        finish_heads(dq, dot(dkv, all_keys[:, :D_LAT]))

    def loop_step():
        row = lax.broadcasted_iota(jnp.int32, (ROWS, TILE), 0)
        col = lax.broadcasted_iota(jnp.int32, (ROWS, TILE), 1)

        def score_tile(t, maxima):
            tile_keys = keys[key_rows(t), :]
            both = dot_nt(tile_keys[:, :D_LAT], wb[...]).astype(BF)
            shown = col <= row + t * (MAX_TILES * TILE)
            new = []
            for h in range(2):
                k_nope = both[:, h * 256 : h * 256 + 128]
                value = both[:, h * 256 + 128 : (h + 1) * 256]
                k_full = jnp.concatenate([k_nope, tile_keys[:, D_LAT:]], axis=1)
                kf[h, t] = k_full
                vv[h, t] = value
                score = jnp.where(shown, dot_nt(qf[h], k_full), HIDE)
                s[h, t] = score
                dp[h, t] = dot_nt(gb[h], value)
                new.append(jnp.maximum(maxima[h], jnp.maximum(score[:, :128], score[:, 128:])))
            return tuple(new)

        low = jnp.full((ROWS, 128), HIDE, F32)
        maxima = each_tile(score_tile, (low, low))
        shifts = [jnp.max(m, axis=1, keepdims=True) * base2 for m in maxima]

        def prob_tile(t, carry):
            new = []
            for h in range(2):
                total, mixed = carry[h]
                expo = jnp.exp2(s[h, t] * base2 - shifts[h])
                total = total + (expo[:, :128] + expo[:, 128:])
                expo = expo.astype(BF)
                e[h, t] = expo
                new.append((total, mixed + dot(expo, vv[h, t])))
            return tuple(new)

        nothing = jnp.zeros((ROWS, 128), F32)
        mixes = each_tile(prob_tile, ((nothing, nothing), (nothing, nothing)))
        slopes, offsets = [], []
        for h in range(2):
            total, mixed = mixes[h]
            inv = 1.0 / jnp.sum(total, axis=1, keepdims=True)
            mixed = mixed * inv
            out[:, h * D_V : (h + 1) * D_V] = mixed.astype(BF)
            g = gb[h].astype(F32)
            row_dot = jnp.sum(mixed * g, axis=1, keepdims=True)
            slopes.append(inv * SCALING)
            offsets.append(row_dot * (inv * SCALING))
            git[h] = (g * inv).astype(BF).T

        wgrad[...] = jnp.zeros(wgrad.shape, F32)

        def back_tile(t, carry):
            tile_keys = keys[key_rows(t), :D_LAT]
            parts, rope_sum, new = [], None, []
            for h in range(2):
                expo = e[h, t]
                ds = (expo.astype(F32) * (dp[h, t] * slopes[h] - offsets[h])).astype(BF)
                new.append(carry[h] + dot(ds, kf[h, t]))
                dk = dot(qt[h], ds)
                dv = dot(git[h], expo)
                parts += [dk[:D_NOPE].astype(BF), dv.astype(BF)]
                rope_sum = dk[D_NOPE:] if h == 0 else rope_sum + dk[D_NOPE:]
            dkv = jnp.concatenate(parts, axis=0)
            add_grads(key_rows(t), dot(wt[...], dkv), rope_sum)
            wgrad[...] += dot(dkv, tile_keys)
            return tuple(new)

        empty = jnp.zeros((ROWS, 256), F32)
        dq = each_tile(back_tile, (empty, empty))
        finish_heads(dq, wgrad[...])

    for count in WIDE:

        @pl.when(tiles == count)
        def _(count=count):
            wide_step(count)

    @pl.when(functools.reduce(lambda x, y: x & y, [tiles != count for count in WIDE]))
    def _():
        loop_step()

    @pl.when(step == pl.num_programs(0) - 1)
    def _():
        chunk, core = info[0], info[1]
        n1, block1, block2, count = meta[1], meta[2], meta[3], meta[4]
        kept[...] = jnp.zeros(kept.shape, BF)
        sent[...] = jnp.zeros(sent.shape, BF)

        def turn(t, carry):
            keys[key_rows(t), :D_LAT] = acc[:D_LAT, key_rows(t)].astype(BF).T
            keys[key_rows(t), D_LAT:] = jnp.concatenate(
                [acc[D_LAT:, key_rows(t)].astype(BF), jnp.zeros((EXTRA - D_ROPE, TILE), BF)], axis=0
            ).T
            return carry

        lax.fori_loop(0, tiles, turn, 0)

        def put(target, slot, y, index):
            target[slot, y] = keys[pl.ds(pl.multiple_of(index * BLOCK, BLOCK), BLOCK), :]

        own_blocks = ROWS // BLOCK
        for y in range(4):
            for target, parity in ((kept, core), (sent, 1 - core)):
                kind = 2 * y + parity
                for i in range(2):
                    put(target, i, y, 8 * i + kind)
                slot = 2
                for start, shift, length in ((block1, 0, n1), (block2, n1, count - n1)):
                    skip = (kind - start) & 7
                    number = jnp.maximum(length - skip + 7, 0) // 8

                    def put_next(i, carry, target=target, y=y, slot=slot, skip=skip, shift=shift):
                        put(target, slot + i, y, own_blocks + shift + skip + 8 * i)
                        return carry

                    lax.fori_loop(0, number, put_next, 0)
                    slot = slot + number


def attention(shared, q_nope, q_rope, d_out, w_uk, w_uv):
    rows = q_nope.shape[0]
    pairs = w_uk.shape[0] // (2 * D_NOPE)

    def columns(size):
        return pl.BlockSpec((rows, size), lambda i: (0, i))

    def heads(size):
        return pl.BlockSpec((size, D_LAT), lambda i: (i, 0))

    whole = pl.BlockSpec(memory_space=pltpu.VMEM)
    in_specs = [pl.BlockSpec(memory_space=pltpu.SMEM)] + [whole] * 5
    in_specs += [columns(256), columns(128), columns(256), heads(256), heads(256)]
    half = jax.ShapeDtypeStruct((SLOTS, 4, BLOCK, PACK), BF)
    return pl.pallas_call(
        attention_kernel,
        grid=(pairs,),
        in_specs=in_specs,
        out_specs=[
            columns(256),
            columns(256),
            columns(128),
            pl.BlockSpec((2, 256, D_LAT), lambda i: (i, 0, 0)),
            whole,
            whole,
            pl.BlockSpec(memory_space=pltpu.SMEM),
        ],
        out_shape=[
            jax.ShapeDtypeStruct(q_nope.shape, BF),
            jax.ShapeDtypeStruct(q_nope.shape, BF),
            jax.ShapeDtypeStruct(q_rope.shape, BF),
            jax.ShapeDtypeStruct((2 * pairs, 256, D_LAT), BF),
            half,
            half,
            jax.ShapeDtypeStruct((8,), jnp.int32),
        ],
        scratch_shapes=[
            pltpu.VMEM((MAX_TILES * TILE, PACK), BF),
            pltpu.VMEM((D_LAT + D_ROPE, MAX_TILES * TILE), F32),
            pltpu.VMEM((2, MAX_TILES, TILE, 256), BF),
            pltpu.VMEM((2, MAX_TILES, TILE, D_V), BF),
            pltpu.VMEM((2, MAX_TILES, ROWS, TILE), F32),
            pltpu.VMEM((2, MAX_TILES, ROWS, TILE), F32),
            pltpu.VMEM((2, MAX_TILES, ROWS, TILE), BF),
            pltpu.VMEM((2, ROWS, 256), BF),
            pltpu.VMEM((2, D_NOPE + D_ROPE, ROWS), BF),
            pltpu.VMEM((2, ROWS, D_V), BF),
            pltpu.VMEM((2, D_V, ROWS), BF),
            pltpu.VMEM((512, D_LAT), BF),
            pltpu.VMEM((D_LAT, 512), BF),
            pltpu.VMEM((512, D_LAT), F32),
        ],
        compiler_params=pltpu.CompilerParams(vmem_limit_bytes=56 << 20),
        cost_estimate=pl.CostEstimate(
            flops=pairs * 2600000000, bytes_accessed=16 << 20, transcendentals=pairs * 400000
        ),
        name="attention",
    )(*shared, q_nope, q_rope, d_out, w_uk, w_uv)


def prepare_kernel(latent, gain, rope_t, gid, cid, gid_s, cid_s, lengths, own, send, bias, weight, inverse, info):
    chunk = lax.axis_index("xl") * 4 + lax.axis_index("z")
    core = lax.axis_index("core")
    latent_f = latent[...].astype(F32)
    inv = lax.rsqrt(jnp.mean(latent_f * latent_f, axis=1, keepdims=True) + 1e-06)
    inverse[...] = inv
    normed = (latent_f * inv * gain[...].astype(F32)[None, :]).astype(BF)
    group = jnp.broadcast_to(gid[...].astype(F32), (8, ROWS)).T[:, :1].astype(jnp.int32)
    comp = jnp.broadcast_to(cid[...].astype(F32), (8, ROWS)).T[:, :1].astype(jnp.int32)
    code = group * (COMP + 1) + comp
    column = lax.broadcasted_iota(jnp.int32, (ROWS, EXTRA - D_ROPE), 1)
    tags = jnp.where(column == code, 1.0, 0.0).astype(BF)
    seen = (column == code) | (column == group * (COMP + 1))
    bias[...] = jnp.where(seen, 0.0, HIDE).astype(BF)
    own[...] = jnp.concatenate([normed, rope_t[...].T, tags], axis=1)
    half = own[pl.ds(pl.multiple_of(core * (ROWS // 2), ROWS // 2), ROWS // 2), :]
    for i in range(CTX):
        send[i] = half
    length = jnp.ones((ROWS, 1), F32)
    for g in range(GROUPS):
        for k in range(COMP):
            length = jnp.where(code == g * (COMP + 1) + k + 1, lengths[g, k].astype(F32), length)
    weight[...] = jnp.where(comp > 0, 64.0 / length, 0.0)
    group0, comp0 = gid_s[0], cid_s[0]
    info[0], info[1], info[2], info[3] = chunk, core, group0, comp0
    info[4] = jnp.sum(
        jnp.where(gid[...] * (COMP + 1) + cid[...] == group0 * (COMP + 1) + comp0, 1.0, 0.0)
    ).astype(jnp.int32)
    info[5] = lengths[group0, jnp.maximum(comp0 - 1, 0)]
    for g in range(GROUPS):
        info[6 + g] = sum([lengths[g, k] for k in range(1, COMP)], lengths[g, 0])


def prepare(latent, latent_gain, k_rope_t, group_ids, comp_ids, comp_lengths):
    vector = pl.BlockSpec(memory_space=LOCAL)
    scalar = pl.BlockSpec(memory_space=pltpu.SMEM)
    return pl.pallas_call(
        prepare_kernel,
        in_specs=[vector] * 5 + [scalar] * 3,
        out_specs=[vector] * 5 + [scalar],
        out_shape=[
            jax.ShapeDtypeStruct((ROWS, PACK), BF),
            jax.ShapeDtypeStruct((CTX, ROWS // 2, PACK), BF),
            jax.ShapeDtypeStruct((ROWS, EXTRA - D_ROPE), BF),
            jax.ShapeDtypeStruct((ROWS, 1), F32),
            jax.ShapeDtypeStruct((ROWS, 1), F32),
            jax.ShapeDtypeStruct((8,), jnp.int32),
        ],
        cost_estimate=SMALL,
        name="prepare",
    )(
        latent,
        latent_gain,
        k_rope_t,
        group_ids[None, :],
        comp_ids[None, :],
        group_ids,
        comp_ids,
        comp_lengths,
    )


def move(x, axis, distance):
    if axis == "x":
        names = ("xl", "xh")
        return lax.ppermute(x, names, [(i, i ^ distance) for i in range(4)])
    return lax.ppermute(x, axis, [(i, (i + distance) % 4) for i in range(4)])


def summed(parts, index):
    total = parts[0][index].astype(F32)
    for part in parts[1:]:
        total = total + part[index].astype(F32)
    return total.astype(BF)


def fold_y_kernel(*refs):
    parts, outs = refs[:2], refs[2:]
    slots = outs[0].shape[0]
    for distance, out in enumerate(outs):
        place = (lax.axis_index("y") + distance) & 3
        for slot in range(slots):
            out[slot] = summed(parts, (slot, place))


def fold_z_kernel(*refs):
    meta, parts, outs = refs[0], refs[1:5], refs[5:9]
    n1, block1, block2, count, chunk = meta[1], meta[2], meta[3], meta[4], meta[5]
    kind = 2 * lax.axis_index("y") + lax.axis_index("core")
    z = lax.axis_index("z")
    spread = refs[9]
    spread[...] = jnp.zeros(spread.shape, BF)

    def put(slot, block):
        pair = block // 8
        spread[(((pair // 2) % 4) - z) & 3, (pair // 8) * 2 + pair % 2] = summed(parts, (slot,))

    for i in range(2):
        put(i, chunk * (ROWS // BLOCK) + 8 * i + kind)
    slot = 2
    for start, length in ((block1, n1), (block2, count - n1)):
        skip = (kind - start) & 7
        number = jnp.maximum(length - skip + 7, 0) // 8

        def put_next(i, carry, slot=slot, first=start + skip):
            put(slot + i, first + 8 * i)
            return carry

        lax.fori_loop(0, number, put_next, 0)
        slot = slot + number
    for distance, out in enumerate(outs):
        out[...] = spread[distance]


def fold_x_kernel(*refs):
    parts, outs = refs[:4], refs[4:]
    for distance, out in enumerate(outs):
        place = lax.axis_index("xl") ^ distance
        for xh in range(2):
            out[xh] = summed(parts, (place * 2 + xh,))


def fold(kernel, operands, cuts, shape, scratch=()):
    vector = pl.BlockSpec(memory_space=LOCAL)
    scalar = pl.BlockSpec(memory_space=pltpu.SMEM)
    return pl.pallas_call(
        kernel,
        in_specs=[scalar if x.dtype == jnp.int32 else vector for x in operands],
        out_specs=[vector] * cuts,
        out_shape=[jax.ShapeDtypeStruct(shape, BF)] * cuts,
        scratch_shapes=scratch,
        cost_estimate=LONG if kernel is fold_y_kernel else SMALL,
        name="fold",
    )(*operands)


def gather_grads(kept, sent, meta, total):
    slots = sent.shape[0]
    cut = fold(fold_y_kernel, [kept, swap_core(sent)], 4, (slots, BLOCK, PACK))
    parts = [cut[0]] + [move(cut[d], "y", d) for d in (2, 1, 3)]
    spread = pltpu.VMEM((4, 4, BLOCK, PACK), BF)
    cut = fold(fold_z_kernel, [meta] + parts, 4, (4, BLOCK, PACK), [spread])
    parts = [cut[0]] + [move(cut[d], "z", d) for d in (2, 1, 3)]
    parts, total = lax.optimization_barrier((parts, total))
    cut = fold(fold_x_kernel, parts, 2, (2, BLOCK, PACK))
    cut, total = lax.optimization_barrier((cut, total))
    return total, [cut[0], move(cut[0], "x", 1), move(cut[1], "x", 2), move(cut[1], "x", 3)]


def finish_kernel(a, b, c, d, latent, inverse, gain, out):
    head = lax.axis_index("y") * 2 + lax.axis_index("core")
    total = sum([part[...].astype(F32) for part in (b, c, d)], a[...].astype(F32))
    total = total.reshape(2 * BLOCK, PACK)
    lifted = total[:, :D_LAT] * gain[...].astype(F32)[None, :]
    places = [pl.ds(pl.multiple_of((xh * 8 + head) * BLOCK, BLOCK), BLOCK) for xh in range(2)]
    own = jnp.concatenate([latent[rows, :] for rows in places], axis=0).astype(F32)
    inv = jnp.concatenate([inverse[rows, :] for rows in places], axis=0)
    centred = jnp.mean(lifted * own, axis=1, keepdims=True)
    out[:, :D_LAT] = (inv * lifted - own * inv**3 * centred).astype(BF)
    out[:, D_LAT:] = total[:, D_LAT:].astype(BF)


def finish(parts, latent, inverse, latent_gain):
    vector = pl.BlockSpec(memory_space=LOCAL)
    return pl.pallas_call(
        finish_kernel,
        in_specs=[vector] * 7,
        out_specs=vector,
        out_shape=jax.ShapeDtypeStruct((2 * BLOCK, PACK), BF),
        cost_estimate=LONG,
        name="finish",
    )(*parts, latent, inverse, latent_gain)


def assemble_kernel(*refs):
    pieces, out, rope, turned = refs[:4], refs[4], refs[5], refs[6]
    y, core = lax.axis_index("y"), lax.axis_index("core")
    for distance, piece in enumerate(pieces):
        for other in range(2):
            for xh in range(2):
                head = xh * 8 + ((y - distance) & 3) * 2 + (core ^ other)
                rows = pl.ds(pl.multiple_of(head * BLOCK, BLOCK), BLOCK)
                place = (other * 2 + xh) * BLOCK
                out[rows, :] = piece[place : place + BLOCK, :D_LAT]
                turned[rows, :] = piece[place : place + BLOCK, D_LAT:].astype(F32)
    rope[...] = turned[...].T[:D_ROPE].astype(BF)


def assemble(pieces):
    vector = pl.BlockSpec(memory_space=LOCAL)
    return pl.pallas_call(
        assemble_kernel,
        in_specs=[vector] * 4,
        out_specs=[vector] * 2,
        out_shape=[
            jax.ShapeDtypeStruct((ROWS, D_LAT), BF),
            jax.ShapeDtypeStruct((D_ROPE, ROWS), BF),
        ],
        scratch_shapes=[pltpu.VMEM((ROWS, EXTRA), F32)],
        cost_estimate=SMALL,
        name="assemble",
    )(*pieces)


def total_kernel(pieces, out, parts, sums, in_sems, out_sems):
    steps = in_sems.shape[0]
    size = sums.shape[0] // steps
    copies = []

    def load(step):
        rows = pl.ds(step * size, size)
        return pltpu.make_async_copy(pieces.at[:, rows, :], parts.at[:, rows, :], in_sems.at[step])

    for step in range(steps):
        load(step).start()
    for step in range(steps):
        load(step).wait()
        rows = pl.ds(step * size, size)
        total = parts[0, rows, :].astype(F32)
        for i in range(1, CTX):
            total = total + parts[i, rows, :].astype(F32)
        sums[rows, :] = total.astype(BF)
        for i in range(CTX):
            copy = pltpu.make_async_copy(sums.at[rows, :], out.at[i, rows, :], out_sems.at[step, i])
            copy.start()
            copies.append(copy)
    for copy in copies:
        copy.wait()


def total_and_copy(pieces):
    anywhere = pl.BlockSpec(memory_space=pl.ANY)
    return pl.pallas_call(
        total_kernel,
        in_specs=[anywhere],
        out_specs=anywhere,
        out_shape=jax.ShapeDtypeStruct(pieces.shape, BF),
        scratch_shapes=[
            pltpu.VMEM(pieces.shape, BF),
            pltpu.VMEM(pieces.shape[1:], BF),
            pltpu.SemaphoreType.DMA((4,)),
            pltpu.SemaphoreType.DMA((4, CTX)),
        ],
        compiler_params=pltpu.CompilerParams(vmem_limit_bytes=62 << 20),
        cost_estimate=SMALL,
        name="total",
    )(pieces)


def swap_core(x):
    return lax.ppermute(x, "core", [(0, 1), (1, 0)])


def exchange(x, axes):
    return lax.all_to_all(x, axes, 0, 0, tiled=True)


def on_device(
    q_nope,
    q_rope,
    latent,
    latent_gain,
    k_rope_t,
    w_uk,
    w_uv,
    d_out,
    group_ids,
    comp_ids,
    comp_lengths,
):
    own, send, bias, weight, inverse, info = prepare(
        latent, latent_gain, k_rope_t, group_ids, comp_ids, comp_lengths
    )
    mine = exchange(send, CTX_AXES).reshape(-1, PACK)
    other = swap_core(mine)
    shared = (info, own, mine, other, bias, weight)
    out, dqn, dqr, dw, kept, sent, meta = attention(shared, q_nope, q_rope, d_out, w_uk, w_uv)
    pieces = exchange(dw, CTX_AXES)
    total = total_and_copy(pieces)
    total, parts = gather_grads(kept, sent, meta, total)
    weights = exchange(total, CTX_AXES)
    final = finish(parts, latent, inverse, latent_gain)
    pair = jnp.concatenate([final, swap_core(final)], axis=0)
    d_latent, d_k_rope_t = assemble([pair] + [move(pair, "y", d) for d in (1, 2, 3)])
    return out, dqn, dqr, d_latent, d_k_rope_t, *[
        weights[:, i * D_NOPE : (i + 1) * D_NOPE].reshape(-1, D_LAT) for i in range(2)
    ]


def solution(mesh):
    fine = Mesh(mesh.devices.reshape(2, 4, 2, 4, 2), CTX_AXES + HEAD_AXES)
    return jax.shard_map(
        on_device,
        mesh=fine,
        in_specs=(
            P(CTX_AXES, HEAD_AXES),
            P(CTX_AXES, HEAD_AXES),
            P(CTX_AXES, None),
            P(),
            P(None, CTX_AXES),
            P(HEAD_AXES, None),
            P(HEAD_AXES, None),
            P(CTX_AXES, HEAD_AXES),
            P(CTX_AXES),
            P(CTX_AXES),
            P(),
        ),
        out_specs=(
            P(CTX_AXES, HEAD_AXES),
            P(CTX_AXES, HEAD_AXES),
            P(CTX_AXES, HEAD_AXES),
            P(CTX_AXES, None),
            P(None, CTX_AXES),
            P(HEAD_AXES, None),
            P(HEAD_AXES, None),
        ),
        check_vma=False,
    )
```

```python
import functools
import math

import jax
import jax.numpy as jnp
from jax import lax
from jax.experimental import pallas as pl
from jax.experimental.pallas import tpu as pltpu
from jax.sharding import Mesh
from jax.sharding import PartitionSpec as P

D_LAT = 512
D_ROPE = 64
D_NOPE = 128
D_V = 128
GROUPS = 2
COMP = 8
CODES = GROUPS * (COMP + 1)
TOKENS = 2048
CTX = 8
ROWS = TOKENS // CTX
BLOCK = 16
TILE = 256
MAX_TILES = 6
HEADS = 4
SLOTS = 12
WIDE = (3, 4)
LONG = pl.CostEstimate(flops=100000000000, bytes_accessed=1, transcendentals=0)
SMALL = pl.CostEstimate(flops=1, bytes_accessed=1, transcendentals=0)
PACK = 640
EXTRA = PACK - D_LAT
PAD_COL = PACK - 1
HIDE = -1e30
SCALING = 1.0 / math.sqrt(D_NOPE + D_ROPE)
BF = jnp.bfloat16
F32 = jnp.float32
CTX_AXES = ("xl", "z")
HEAD_AXES = ("xh", "y", "core")
LOCAL = pltpu.VMEM


def dot(a, b):
    return lax.dot_general(a, b, (((1,), (0,)), ((), ())), preferred_element_type=F32)


def dot_nt(a, b):
    return lax.dot_general(a, b, (((1,), (1,)), ((), ())), preferred_element_type=F32)


def attention_kernel(*refs):
    info, own, mine, other, bias, weight, qn, qr, do, wk, wv = refs[:11]
    out, dqn, dqr, dw, kept, sent, meta = refs[11:18]
    keys, acc, kf, vv, s, dp, e, qf, qt, gb, git, wb, wt, wgrad = refs[18:]
    step = pl.program_id(0)

    def key_rows(t):
        return pl.ds(pl.multiple_of(t * TILE, TILE), TILE)

    @pl.when(step == 0)
    def _():
        chunk, core, group, comp = info[0], info[1], info[2], info[3]
        inside, length, len0, len1 = info[4], info[5], info[6], info[7]
        tags = jnp.sum(
            mine[:, D_LAT:].astype(F32) + other[:, D_LAT:].astype(F32), axis=0, keepdims=True
        )
        lane = lax.broadcasted_iota(jnp.int32, tags.shape, 1) - D_ROPE
        start1 = jnp.sum(jnp.where((lane >= 0) & (lane < COMP + 1), tags, 0.0)).astype(jnp.int32)
        begin = chunk * ROWS
        low1 = jnp.where(group == 0, 0, start1)
        high1 = jnp.minimum(jnp.where(group == 0, start1 - len0, TOKENS - len1), begin)
        block1 = low1 // BLOCK
        n1 = jnp.where(high1 > low1, (high1 + BLOCK - 1) // BLOCK - block1, 0)
        prior = jnp.where(comp > 0, length - inside, 0)
        block2 = jnp.maximum((begin - prior) // BLOCK, jnp.where(n1 > 0, block1 + n1, 0))
        count = n1 + jnp.maximum(begin // BLOCK - block2, 0)
        count = jnp.minimum(count, (MAX_TILES - 1) * (TILE // BLOCK))
        tiles = 1 + (count + TILE // BLOCK - 1) // (TILE // BLOCK)
        meta[0], meta[1], meta[2], meta[3], meta[4] = tiles, n1, block1, block2, count
        meta[5] = chunk
        keys[0:ROWS, :] = own[...]

        def copy_block(index, carry):
            block = jnp.where(index < n1, block1 + index, block2 + index - n1)
            place = (block // 16) * 8 + block % 8
            rows = pl.ds(pl.multiple_of(place * BLOCK, BLOCK), BLOCK)
            from_mine = ((block % 16) // 8 == core).astype(jnp.int32)
            keys[pl.ds(pl.multiple_of(ROWS + index * BLOCK, BLOCK), BLOCK), :] = jnp.where(
                from_mine == 1, mine[rows, :], other[rows, :]
            )
            return carry

        lax.fori_loop(0, count, copy_block, 0)
        filler = (lax.broadcasted_iota(jnp.int32, (BLOCK, PACK), 1) == PAD_COL).astype(F32).astype(BF)

        def pad_block(index, carry):
            keys[pl.ds(pl.multiple_of(ROWS + index * BLOCK, BLOCK), BLOCK), :] = filler
            return carry

        lax.fori_loop(count, (tiles - 1) * (TILE // BLOCK), pad_block, 0)

        def start_acc(t, carry):
            acc[:, key_rows(t)] = jnp.zeros((acc.shape[0], TILE), F32)
            return carry

        lax.fori_loop(0, tiles, start_acc, 0)

    tiles = meta[0]

    def each_tile(body, carry):
        return lax.fori_loop(0, tiles, body, carry)

    row_weight = weight[...]
    for h in range(HEADS):
        nope = qn[:, h * D_NOPE : (h + 1) * D_NOPE]
        rope = qr[:, h * D_ROPE : (h + 1) * D_ROPE]
        qf[h] = jnp.concatenate([nope, rope, bias[...]], axis=1)
        qt[h] = jnp.concatenate([nope.T, rope.T], axis=0)
        gb[h] = (do[:, h * D_V : (h + 1) * D_V].astype(F32) * row_weight).astype(BF)
        w_head = jnp.concatenate(
            [wk[h * D_NOPE : (h + 1) * D_NOPE, :], wv[h * D_V : (h + 1) * D_V, :]], axis=0
        )
        wb[h * 256 : (h + 1) * 256, :] = w_head
        wt[:, h * 256 : (h + 1) * 256] = w_head.T

    base2 = SCALING * math.log2(math.e)

    def add_grads(cols, lat_grads, rope_grads):
        acc[:D_LAT, cols] += lat_grads
        acc[D_LAT:, cols] += rope_grads

    def finish_heads(dq, grad):
        for h in range(HEADS):
            dqn[:, h * D_NOPE : (h + 1) * D_NOPE] = dq[h][:, :D_NOPE].astype(BF)
            dw[h] = grad[h * 256 : (h + 1) * 256].astype(BF)
        dqr[...] = jnp.concatenate(
            [dq[h][:, D_NOPE : D_NOPE + D_ROPE] for h in range(HEADS)], axis=1
        ).astype(BF)

    def wide_step(count):
        width = count * TILE
        all_keys = keys[:width, :]
        both = dot_nt(all_keys[:, :D_LAT], wb[...]).astype(BF)
        shown = lax.broadcasted_iota(jnp.int32, (ROWS, TILE), 1) <= lax.broadcasted_iota(
            jnp.int32, (ROWS, TILE), 0
        )
        heads = range(HEADS)
        parts, rope_sum, dq = [], None, []
        k_fulls = [jnp.concatenate([both[:, h * 256 : h * 256 + 128], all_keys[:, D_LAT:]], axis=1) for h in heads]
        values = [both[:, h * 256 + 128 : (h + 1) * 256] for h in heads]
        scores = [dot_nt(qf[h], k_fulls[h]) for h in heads]
        scores = [jnp.concatenate([jnp.where(shown, x[:, :TILE], HIDE), x[:, TILE:]], axis=1) for x in scores]
        dprobs = [dot_nt(gb[h], values[h]) for h in heads]
        expos = [jnp.exp2(x * base2 - jnp.max(x, axis=1, keepdims=True) * base2) for x in scores]
        invs = [1.0 / jnp.sum(x, axis=1, keepdims=True) for x in expos]
        expos = [x.astype(BF) for x in expos]
        mixes = [dot(expos[h], values[h]) * invs[h] for h in heads]
        gs = [gb[h].astype(F32) for h in heads]
        dvs = [dot((gs[h] * invs[h]).astype(BF).T, expos[h]) for h in heads]
        dss = []
        for h in heads:
            out[:, h * D_V : (h + 1) * D_V] = mixes[h].astype(BF)
            slope = invs[h] * SCALING
            offset = jnp.sum(mixes[h] * gs[h], axis=1, keepdims=True) * slope
            dss.append((expos[h].astype(F32) * (dprobs[h] * slope - offset)).astype(BF))
        dks = [dot(qt[h], dss[h]) for h in heads]
        dq = [dot(dss[h], k_fulls[h]) for h in heads]
        for h in heads:
            parts += [dks[h][:D_NOPE].astype(BF), dvs[h].astype(BF)]
        rope_sum = sum([x[D_NOPE:] for x in dks[1:]], dks[0][D_NOPE:])
        dkv = jnp.concatenate(parts, axis=0)
        add_grads(slice(0, width), dot(wt[...], dkv), rope_sum)
        finish_heads(dq, dot(dkv, all_keys[:, :D_LAT]))

    def loop_step():
        row = lax.broadcasted_iota(jnp.int32, (ROWS, TILE), 0)
        col = lax.broadcasted_iota(jnp.int32, (ROWS, TILE), 1)

        def score_tile(t, maxima):
            tile_keys = keys[key_rows(t), :]
            both = dot_nt(tile_keys[:, :D_LAT], wb[...]).astype(BF)
            shown = col <= row + t * (MAX_TILES * TILE)
            new = []
            for h in range(HEADS):
                k_nope = both[:, h * 256 : h * 256 + 128]
                value = both[:, h * 256 + 128 : (h + 1) * 256]
                k_full = jnp.concatenate([k_nope, tile_keys[:, D_LAT:]], axis=1)
                kf[h, t] = k_full
                vv[h, t] = value
                score = jnp.where(shown, dot_nt(qf[h], k_full), HIDE)
                s[h, t] = score
                dp[h, t] = dot_nt(gb[h], value)
                new.append(jnp.maximum(maxima[h], jnp.maximum(score[:, :128], score[:, 128:])))
            return tuple(new)

        low = jnp.full((ROWS, 128), HIDE, F32)
        maxima = each_tile(score_tile, (low,) * HEADS)
        shifts = [jnp.max(m, axis=1, keepdims=True) * base2 for m in maxima]

        def prob_tile(t, carry):
            new = []
            for h in range(HEADS):
                total, mixed = carry[h]
                expo = jnp.exp2(s[h, t] * base2 - shifts[h])
                total = total + (expo[:, :128] + expo[:, 128:])
                expo = expo.astype(BF)
                e[h, t] = expo
                new.append((total, mixed + dot(expo, vv[h, t])))
            return tuple(new)

        nothing = jnp.zeros((ROWS, 128), F32)
        mixes = each_tile(prob_tile, ((nothing, nothing),) * HEADS)
        slopes, offsets = [], []
        for h in range(HEADS):
            total, mixed = mixes[h]
            inv = 1.0 / jnp.sum(total, axis=1, keepdims=True)
            mixed = mixed * inv
            out[:, h * D_V : (h + 1) * D_V] = mixed.astype(BF)
            g = gb[h].astype(F32)
            row_dot = jnp.sum(mixed * g, axis=1, keepdims=True)
            slopes.append(inv * SCALING)
            offsets.append(row_dot * (inv * SCALING))
            git[h] = (g * inv).astype(BF).T

        wgrad[...] = jnp.zeros(wgrad.shape, F32)

        def back_tile(t, carry):
            tile_keys = keys[key_rows(t), :D_LAT]
            parts, rope_sum, new = [], None, []
            for h in range(HEADS):
                expo = e[h, t]
                ds = (expo.astype(F32) * (dp[h, t] * slopes[h] - offsets[h])).astype(BF)
                new.append(carry[h] + dot(ds, kf[h, t]))
                dk = dot(qt[h], ds)
                dv = dot(git[h], expo)
                parts += [dk[:D_NOPE].astype(BF), dv.astype(BF)]
                rope_sum = dk[D_NOPE:] if h == 0 else rope_sum + dk[D_NOPE:]
            dkv = jnp.concatenate(parts, axis=0)
            add_grads(key_rows(t), dot(wt[...], dkv), rope_sum)
            wgrad[...] += dot(dkv, tile_keys)
            return tuple(new)

        empty = jnp.zeros((ROWS, 256), F32)
        dq = each_tile(back_tile, (empty,) * HEADS)
        finish_heads(dq, wgrad[...])

    for count in WIDE:

        @pl.when(tiles == count)
        def _(count=count):
            wide_step(count)

    @pl.when(functools.reduce(lambda x, y: x & y, [tiles != count for count in WIDE]))
    def _():
        loop_step()

    @pl.when(step == pl.num_programs(0) - 1)
    def _():
        chunk, core = info[0], info[1]
        n1, block1, block2, count = meta[1], meta[2], meta[3], meta[4]
        kept[...] = jnp.zeros(kept.shape, BF)
        sent[...] = jnp.zeros(sent.shape, BF)

        def turn(t, carry):
            keys[key_rows(t), :D_LAT] = acc[:D_LAT, key_rows(t)].astype(BF).T
            keys[key_rows(t), D_LAT:] = jnp.concatenate(
                [acc[D_LAT:, key_rows(t)].astype(BF), jnp.zeros((EXTRA - D_ROPE, TILE), BF)], axis=0
            ).T
            return carry

        lax.fori_loop(0, tiles, turn, 0)

        def put(target, slot, y, index):
            target[slot, y] = keys[pl.ds(pl.multiple_of(index * BLOCK, BLOCK), BLOCK), :]

        own_blocks = ROWS // BLOCK
        for y in range(4):
            for target, parity in ((kept, core), (sent, 1 - core)):
                kind = 2 * y + parity
                for i in range(2):
                    put(target, i, y, 8 * i + kind)
                slot = 2
                for start, shift, length in ((block1, 0, n1), (block2, n1, count - n1)):
                    skip = (kind - start) & 7
                    number = jnp.maximum(length - skip + 7, 0) // 8

                    def put_next(i, carry, target=target, y=y, slot=slot, skip=skip, shift=shift):
                        put(target, slot + i, y, own_blocks + shift + skip + 8 * i)
                        return carry

                    lax.fori_loop(0, number, put_next, 0)
                    slot = slot + number


def attention(shared, q_nope, q_rope, d_out, w_uk, w_uv):
    rows = q_nope.shape[0]
    pairs = w_uk.shape[0] // (HEADS * D_NOPE)

    def columns(size):
        return pl.BlockSpec((rows, size), lambda i: (0, i))

    def heads(size):
        return pl.BlockSpec((size, D_LAT), lambda i: (i, 0))

    whole = pl.BlockSpec(memory_space=pltpu.VMEM)
    in_specs = [pl.BlockSpec(memory_space=pltpu.SMEM)] + [whole] * 5
    in_specs += [columns(HEADS * D_NOPE), columns(HEADS * D_ROPE), columns(HEADS * D_V), heads(HEADS * D_NOPE), heads(HEADS * D_V)]
    half = jax.ShapeDtypeStruct((SLOTS, 4, BLOCK, PACK), BF)
    return pl.pallas_call(
        attention_kernel,
        grid=(pairs,),
        in_specs=in_specs,
        out_specs=[
            columns(HEADS * D_V),
            columns(HEADS * D_NOPE),
            columns(HEADS * D_ROPE),
            pl.BlockSpec((HEADS, 256, D_LAT), lambda i: (i, 0, 0)),
            whole,
            whole,
            pl.BlockSpec(memory_space=pltpu.SMEM),
        ],
        out_shape=[
            jax.ShapeDtypeStruct(q_nope.shape, BF),
            jax.ShapeDtypeStruct(q_nope.shape, BF),
            jax.ShapeDtypeStruct(q_rope.shape, BF),
            jax.ShapeDtypeStruct((HEADS * pairs, 256, D_LAT), BF),
            half,
            half,
            jax.ShapeDtypeStruct((8,), jnp.int32),
        ],
        scratch_shapes=[
            pltpu.VMEM((MAX_TILES * TILE, PACK), BF),
            pltpu.VMEM((D_LAT + D_ROPE, MAX_TILES * TILE), F32),
            pltpu.VMEM((HEADS, MAX_TILES, TILE, 256), BF),
            pltpu.VMEM((HEADS, MAX_TILES, TILE, D_V), BF),
            pltpu.VMEM((HEADS, MAX_TILES, ROWS, TILE), F32),
            pltpu.VMEM((HEADS, MAX_TILES, ROWS, TILE), F32),
            pltpu.VMEM((HEADS, MAX_TILES, ROWS, TILE), BF),
            pltpu.VMEM((HEADS, ROWS, 256), BF),
            pltpu.VMEM((HEADS, D_NOPE + D_ROPE, ROWS), BF),
            pltpu.VMEM((HEADS, ROWS, D_V), BF),
            pltpu.VMEM((HEADS, D_V, ROWS), BF),
            pltpu.VMEM((HEADS * 256, D_LAT), BF),
            pltpu.VMEM((D_LAT, HEADS * 256), BF),
            pltpu.VMEM((HEADS * 256, D_LAT), F32),
        ],
        compiler_params=pltpu.CompilerParams(vmem_limit_bytes=56 << 20),
        cost_estimate=pl.CostEstimate(
            flops=pairs * HEADS * 1300000000, bytes_accessed=16 << 20, transcendentals=pairs * 400000
        ),
        name="attention",
    )(*shared, q_nope, q_rope, d_out, w_uk, w_uv)


def prepare_kernel(latent, gain, rope_t, gid, cid, gid_s, cid_s, lengths, own, send, bias, weight, inverse, info):
    chunk = lax.axis_index("xl") * 4 + lax.axis_index("z")
    core = lax.axis_index("core")
    latent_f = latent[...].astype(F32)
    inv = lax.rsqrt(jnp.mean(latent_f * latent_f, axis=1, keepdims=True) + 1e-06)
    inverse[...] = inv
    normed = (latent_f * inv * gain[...].astype(F32)[None, :]).astype(BF)
    group = jnp.broadcast_to(gid[...].astype(F32), (8, ROWS)).T[:, :1].astype(jnp.int32)
    comp = jnp.broadcast_to(cid[...].astype(F32), (8, ROWS)).T[:, :1].astype(jnp.int32)
    code = group * (COMP + 1) + comp
    column = lax.broadcasted_iota(jnp.int32, (ROWS, EXTRA - D_ROPE), 1)
    tags = jnp.where(column == code, 1.0, 0.0).astype(BF)
    seen = (column == code) | (column == group * (COMP + 1))
    bias[...] = jnp.where(seen, 0.0, HIDE).astype(BF)
    own[...] = jnp.concatenate([normed, rope_t[...].T, tags], axis=1)
    half = own[pl.ds(pl.multiple_of(core * (ROWS // 2), ROWS // 2), ROWS // 2), :]
    for i in range(CTX):
        send[i] = half
    length = jnp.ones((ROWS, 1), F32)
    for g in range(GROUPS):
        for k in range(COMP):
            length = jnp.where(code == g * (COMP + 1) + k + 1, lengths[g, k].astype(F32), length)
    weight[...] = jnp.where(comp > 0, 64.0 / length, 0.0)
    group0, comp0 = gid_s[0], cid_s[0]
    info[0], info[1], info[2], info[3] = chunk, core, group0, comp0
    info[4] = jnp.sum(
        jnp.where(gid[...] * (COMP + 1) + cid[...] == group0 * (COMP + 1) + comp0, 1.0, 0.0)
    ).astype(jnp.int32)
    info[5] = lengths[group0, jnp.maximum(comp0 - 1, 0)]
    for g in range(GROUPS):
        info[6 + g] = sum([lengths[g, k] for k in range(1, COMP)], lengths[g, 0])


def prepare(latent, latent_gain, k_rope_t, group_ids, comp_ids, comp_lengths):
    vector = pl.BlockSpec(memory_space=LOCAL)
    scalar = pl.BlockSpec(memory_space=pltpu.SMEM)
    return pl.pallas_call(
        prepare_kernel,
        in_specs=[vector] * 5 + [scalar] * 3,
        out_specs=[vector] * 5 + [scalar],
        out_shape=[
            jax.ShapeDtypeStruct((ROWS, PACK), BF),
            jax.ShapeDtypeStruct((CTX, ROWS // 2, PACK), BF),
            jax.ShapeDtypeStruct((ROWS, EXTRA - D_ROPE), BF),
            jax.ShapeDtypeStruct((ROWS, 1), F32),
            jax.ShapeDtypeStruct((ROWS, 1), F32),
            jax.ShapeDtypeStruct((8,), jnp.int32),
        ],
        cost_estimate=SMALL,
        name="prepare",
    )(
        latent,
        latent_gain,
        k_rope_t,
        group_ids[None, :],
        comp_ids[None, :],
        group_ids,
        comp_ids,
        comp_lengths,
    )


def move(x, axis, distance):
    if axis == "x":
        names = ("xl", "xh")
        return lax.ppermute(x, names, [(i, i ^ distance) for i in range(4)])
    return lax.ppermute(x, axis, [(i, (i + distance) % 4) for i in range(4)])


def summed(parts, index):
    total = parts[0][index].astype(F32)
    for part in parts[1:]:
        total = total + part[index].astype(F32)
    return total.astype(BF)


def fold_y_kernel(*refs):
    parts, outs = refs[:2], refs[2:]
    slots = outs[0].shape[0]
    for distance, out in enumerate(outs):
        place = (lax.axis_index("y") + distance) & 3
        for slot in range(slots):
            out[slot] = summed(parts, (slot, place))


def fold_z_kernel(*refs):
    meta, parts, outs = refs[0], refs[1:5], refs[5:9]
    n1, block1, block2, count, chunk = meta[1], meta[2], meta[3], meta[4], meta[5]
    kind = 2 * lax.axis_index("y") + lax.axis_index("core")
    z = lax.axis_index("z")
    spread = refs[9]
    spread[...] = jnp.zeros(spread.shape, BF)

    def put(slot, block):
        pair = block // 8
        spread[(((pair // 2) % 4) - z) & 3, (pair // 8) * 2 + pair % 2] = summed(parts, (slot,))

    for i in range(2):
        put(i, chunk * (ROWS // BLOCK) + 8 * i + kind)
    slot = 2
    for start, length in ((block1, n1), (block2, count - n1)):
        skip = (kind - start) & 7
        number = jnp.maximum(length - skip + 7, 0) // 8

        def put_next(i, carry, slot=slot, first=start + skip):
            put(slot + i, first + 8 * i)
            return carry

        lax.fori_loop(0, number, put_next, 0)
        slot = slot + number
    for distance, out in enumerate(outs):
        out[...] = spread[distance]


def fold(kernel, operands, cuts, shape, scratch=()):
    vector = pl.BlockSpec(memory_space=LOCAL)
    scalar = pl.BlockSpec(memory_space=pltpu.SMEM)
    return pl.pallas_call(
        kernel,
        in_specs=[scalar if x.dtype == jnp.int32 else vector for x in operands],
        out_specs=[vector] * cuts,
        out_shape=[jax.ShapeDtypeStruct(shape, BF)] * cuts,
        scratch_shapes=scratch,
        cost_estimate=LONG if kernel is fold_y_kernel else SMALL,
        name="fold",
    )(*operands)


def gather_grads(kept, sent, meta, total):
    slots = sent.shape[0]
    cut = fold(fold_y_kernel, [kept, swap_core(sent)], 4, (slots, BLOCK, PACK))
    parts = [cut[0]] + [move(cut[d], "y", d) for d in (2, 1, 3)]
    spread = pltpu.VMEM((4, 4, BLOCK, PACK), BF)
    cut = fold(fold_z_kernel, [meta] + parts, 4, (4, BLOCK, PACK), [spread])
    parts = [cut[0]] + [move(cut[d], "z", d) for d in (2, 1, 3)]
    parts, total = lax.optimization_barrier((parts, total))
    part = sum([x.astype(F32) for x in parts[1:]], parts[0].astype(F32)).astype(BF)
    part, total = lax.optimization_barrier((part, total))
    return total, [part] + [move(part, "x", d) for d in (1, 2, 3)]


def finish_kernel(a, b, c, d, latent, inverse, gain, out):
    head = lax.axis_index("y") * 2 + lax.axis_index("core")
    blocks = pl.ds(lax.axis_index("xl") * 2, 2)
    total = sum([part[blocks].astype(F32) for part in (b, c, d)], a[blocks].astype(F32))
    total = total.reshape(2 * BLOCK, PACK)
    lifted = total[:, :D_LAT] * gain[...].astype(F32)[None, :]
    places = [pl.ds(pl.multiple_of((xh * 8 + head) * BLOCK, BLOCK), BLOCK) for xh in range(2)]
    own = jnp.concatenate([latent[rows, :] for rows in places], axis=0).astype(F32)
    inv = jnp.concatenate([inverse[rows, :] for rows in places], axis=0)
    centred = jnp.mean(lifted * own, axis=1, keepdims=True)
    out[:, :D_LAT] = (inv * lifted - own * inv**3 * centred).astype(BF)
    out[:, D_LAT:] = total[:, D_LAT:].astype(BF)


def finish(parts, latent, inverse, latent_gain):
    vector = pl.BlockSpec(memory_space=LOCAL)
    return pl.pallas_call(
        finish_kernel,
        in_specs=[vector] * 7,
        out_specs=vector,
        out_shape=jax.ShapeDtypeStruct((2 * BLOCK, PACK), BF),
        cost_estimate=LONG,
        name="finish",
    )(*parts, latent, inverse, latent_gain)


def assemble_kernel(*refs):
    pieces, out, rope, turned = refs[:4], refs[4], refs[5], refs[6]
    y, core = lax.axis_index("y"), lax.axis_index("core")
    for distance, piece in enumerate(pieces):
        for other in range(2):
            for xh in range(2):
                head = xh * 8 + ((y - distance) & 3) * 2 + (core ^ other)
                rows = pl.ds(pl.multiple_of(head * BLOCK, BLOCK), BLOCK)
                place = (other * 2 + xh) * BLOCK
                out[rows, :] = piece[place : place + BLOCK, :D_LAT]
                turned[rows, :] = piece[place : place + BLOCK, D_LAT:].astype(F32)
    rope[...] = turned[...].T[:D_ROPE].astype(BF)


def assemble(pieces):
    vector = pl.BlockSpec(memory_space=LOCAL)
    return pl.pallas_call(
        assemble_kernel,
        in_specs=[vector] * 4,
        out_specs=[vector] * 2,
        out_shape=[
            jax.ShapeDtypeStruct((ROWS, D_LAT), BF),
            jax.ShapeDtypeStruct((D_ROPE, ROWS), BF),
        ],
        scratch_shapes=[pltpu.VMEM((ROWS, EXTRA), F32)],
        cost_estimate=SMALL,
        name="assemble",
    )(*pieces)


def total_kernel(pieces, out, parts, sums, in_sems, out_sems):
    steps = in_sems.shape[0]
    size = sums.shape[0] // steps
    copies = []

    def load(step):
        rows = pl.ds(step * size, size)
        return pltpu.make_async_copy(pieces.at[:, rows, :], parts.at[:, rows, :], in_sems.at[step])

    for step in range(steps):
        load(step).start()
    for step in range(steps):
        load(step).wait()
        rows = pl.ds(step * size, size)
        total = parts[0, rows, :].astype(F32)
        for i in range(1, CTX):
            total = total + parts[i, rows, :].astype(F32)
        sums[rows, :] = total.astype(BF)
        for i in range(CTX):
            copy = pltpu.make_async_copy(sums.at[rows, :], out.at[i, rows, :], out_sems.at[step, i])
            copy.start()
            copies.append(copy)
    for copy in copies:
        copy.wait()


def total_and_copy(pieces):
    anywhere = pl.BlockSpec(memory_space=pl.ANY)
    return pl.pallas_call(
        total_kernel,
        in_specs=[anywhere],
        out_specs=anywhere,
        out_shape=jax.ShapeDtypeStruct(pieces.shape, BF),
        scratch_shapes=[
            pltpu.VMEM(pieces.shape, BF),
            pltpu.VMEM(pieces.shape[1:], BF),
            pltpu.SemaphoreType.DMA((4,)),
            pltpu.SemaphoreType.DMA((4, CTX)),
        ],
        compiler_params=pltpu.CompilerParams(vmem_limit_bytes=62 << 20),
        cost_estimate=SMALL,
        name="total",
    )(pieces)


def swap_core(x):
    return lax.ppermute(x, "core", [(0, 1), (1, 0)])


def exchange(x, axes):
    return lax.all_to_all(x, axes, 0, 0, tiled=True)


def on_device(
    q_nope,
    q_rope,
    latent,
    latent_gain,
    k_rope_t,
    w_uk,
    w_uv,
    d_out,
    group_ids,
    comp_ids,
    comp_lengths,
):
    own, send, bias, weight, inverse, info = prepare(
        latent, latent_gain, k_rope_t, group_ids, comp_ids, comp_lengths
    )
    mine = exchange(send, CTX_AXES).reshape(-1, PACK)
    other = swap_core(mine)
    shared = (info, own, mine, other, bias, weight)
    out, dqn, dqr, dw, kept, sent, meta = attention(shared, q_nope, q_rope, d_out, w_uk, w_uv)
    pieces = exchange(dw, CTX_AXES)
    total = total_and_copy(pieces)
    total, parts = gather_grads(kept, sent, meta, total)
    weights = exchange(total, CTX_AXES)
    final = finish(parts, latent, inverse, latent_gain)
    pair = jnp.concatenate([final, swap_core(final)], axis=0)
    d_latent, d_k_rope_t = assemble([pair] + [move(pair, "y", d) for d in (1, 2, 3)])
    return out, dqn, dqr, d_latent, d_k_rope_t, *[
        weights[:, i * D_NOPE : (i + 1) * D_NOPE].reshape(-1, D_LAT) for i in range(2)
    ]


def solution(mesh):
    fine = Mesh(mesh.devices.reshape(2, 4, 2, 4, 2), CTX_AXES + HEAD_AXES)
    return jax.shard_map(
        on_device,
        mesh=fine,
        in_specs=(
            P(CTX_AXES, HEAD_AXES),
            P(CTX_AXES, HEAD_AXES),
            P(CTX_AXES, None),
            P(),
            P(None, CTX_AXES),
            P(HEAD_AXES, None),
            P(HEAD_AXES, None),
            P(CTX_AXES, HEAD_AXES),
            P(CTX_AXES),
            P(CTX_AXES),
            P(),
        ),
        out_specs=(
            P(CTX_AXES, HEAD_AXES),
            P(CTX_AXES, HEAD_AXES),
            P(CTX_AXES, HEAD_AXES),
            P(CTX_AXES, None),
            P(None, CTX_AXES),
            P(HEAD_AXES, None),
            P(HEAD_AXES, None),
        ),
        check_vma=False,
    )
```

```python
import functools
import math

import jax
import jax.numpy as jnp
from jax import lax
from jax.experimental import pallas as pl
from jax.experimental.pallas import tpu as pltpu
from jax.sharding import Mesh
from jax.sharding import PartitionSpec as P

D_LAT = 512
D_ROPE = 64
D_NOPE = 128
D_V = 128
GROUPS = 2
COMP = 8
CODES = GROUPS * (COMP + 1)
TOKENS = 2048
CTX = 8
ROWS = TOKENS // CTX
BLOCK = 16
TILE = 256
MAX_TILES = 6
HEADS = 4
SLOTS = 12
WIDE = (3, 4)
LONG = pl.CostEstimate(flops=100000000000, bytes_accessed=1, transcendentals=0)
SMALL = pl.CostEstimate(flops=1, bytes_accessed=1, transcendentals=0)
PACK = 640
EXTRA = PACK - D_LAT
PAD_COL = PACK - 1
HIDE = -1e30
SCALING = 1.0 / math.sqrt(D_NOPE + D_ROPE)
BF = jnp.bfloat16
F32 = jnp.float32
CTX_AXES = ("xl", "z")
HEAD_AXES = ("xh", "y", "core")
LOCAL = pltpu.VMEM


def dot(a, b):
    return lax.dot_general(a, b, (((1,), (0,)), ((), ())), preferred_element_type=F32)


def dot_nt(a, b):
    return lax.dot_general(a, b, (((1,), (1,)), ((), ())), preferred_element_type=F32)


def attention_kernel(*refs):
    info, own, mine, other, bias, weight, qn, qr, do, wk, wv = refs[:11]
    out, dqn, dqr, dw, kept, sent, meta = refs[11:18]
    keys, acc, kf, vv, s, dp, e, qf, qt, gb, git, wb, wt, wgrad = refs[18:]
    step = pl.program_id(0)

    def key_rows(t):
        return pl.ds(pl.multiple_of(t * TILE, TILE), TILE)

    @pl.when(step == 0)
    def _():
        chunk, core, group, comp = info[0], info[1], info[2], info[3]
        inside, length, len0, len1 = info[4], info[5], info[6], info[7]
        tags = jnp.sum(
            mine[:, D_LAT:].astype(F32) + other[:, D_LAT:].astype(F32), axis=0, keepdims=True
        )
        lane = lax.broadcasted_iota(jnp.int32, tags.shape, 1) - D_ROPE
        start1 = jnp.sum(jnp.where((lane >= 0) & (lane < COMP + 1), tags, 0.0)).astype(jnp.int32)
        begin = chunk * ROWS
        low1 = jnp.where(group == 0, 0, start1)
        high1 = jnp.minimum(jnp.where(group == 0, start1 - len0, TOKENS - len1), begin)
        block1 = low1 // BLOCK
        n1 = jnp.where(high1 > low1, (high1 + BLOCK - 1) // BLOCK - block1, 0)
        prior = jnp.where(comp > 0, length - inside, 0)
        block2 = jnp.maximum((begin - prior) // BLOCK, jnp.where(n1 > 0, block1 + n1, 0))
        count = n1 + jnp.maximum(begin // BLOCK - block2, 0)
        count = jnp.minimum(count, (MAX_TILES - 1) * (TILE // BLOCK))
        tiles = 1 + (count + TILE // BLOCK - 1) // (TILE // BLOCK)
        meta[0], meta[1], meta[2], meta[3], meta[4] = tiles, n1, block1, block2, count
        meta[5] = chunk
        keys[0:ROWS, :] = own[...]

        def copy_block(index, carry):
            block = jnp.where(index < n1, block1 + index, block2 + index - n1)
            place = (block // 16) * 8 + block % 8
            rows = pl.ds(pl.multiple_of(place * BLOCK, BLOCK), BLOCK)
            from_mine = ((block % 16) // 8 == core).astype(jnp.int32)
            keys[pl.ds(pl.multiple_of(ROWS + index * BLOCK, BLOCK), BLOCK), :] = jnp.where(
                from_mine == 1, mine[rows, :], other[rows, :]
            )
            return carry

        lax.fori_loop(0, count, copy_block, 0)
        filler = (lax.broadcasted_iota(jnp.int32, (BLOCK, PACK), 1) == PAD_COL).astype(F32).astype(BF)

        def pad_block(index, carry):
            keys[pl.ds(pl.multiple_of(ROWS + index * BLOCK, BLOCK), BLOCK), :] = filler
            return carry

        lax.fori_loop(count, (tiles - 1) * (TILE // BLOCK), pad_block, 0)

        def start_acc(t, carry):
            acc[:, key_rows(t)] = jnp.zeros((acc.shape[0], TILE), F32)
            return carry

        lax.fori_loop(0, tiles, start_acc, 0)

    tiles = meta[0]

    def each_tile(body, carry):
        return lax.fori_loop(0, tiles, body, carry)

    row_weight = weight[...]
    for h in range(HEADS):
        nope = qn[:, h * D_NOPE : (h + 1) * D_NOPE]
        rope = qr[:, h * D_ROPE : (h + 1) * D_ROPE]
        qf[h] = jnp.concatenate([nope, rope, bias[...]], axis=1)
        qt[h] = jnp.concatenate([nope.T, rope.T], axis=0)
        gb[h] = (do[:, h * D_V : (h + 1) * D_V].astype(F32) * row_weight).astype(BF)
        w_head = jnp.concatenate(
            [wk[h * D_NOPE : (h + 1) * D_NOPE, :], wv[h * D_V : (h + 1) * D_V, :]], axis=0
        )
        wb[h * 256 : (h + 1) * 256, :] = w_head
        wt[:, h * 256 : (h + 1) * 256] = w_head.T

    base2 = SCALING * math.log2(math.e)

    def add_grads(cols, lat_grads, rope_grads):
        acc[:D_LAT, cols] += lat_grads
        acc[D_LAT:, cols] += rope_grads

    def finish_heads(dq, grad):
        for h in range(HEADS):
            dqn[:, h * D_NOPE : (h + 1) * D_NOPE] = dq[h][:, :D_NOPE].astype(BF)
            dw[h] = grad[h * 256 : (h + 1) * 256].astype(BF)
        dqr[...] = jnp.concatenate(
            [dq[h][:, D_NOPE : D_NOPE + D_ROPE] for h in range(HEADS)], axis=1
        ).astype(BF)

    def wide_step(count):
        width = count * TILE
        all_keys = keys[:width, :]
        both = dot_nt(all_keys[:, :D_LAT], wb[...]).astype(BF)
        shown = lax.broadcasted_iota(jnp.int32, (ROWS, TILE), 1) <= lax.broadcasted_iota(
            jnp.int32, (ROWS, TILE), 0
        )
        heads = range(HEADS)
        parts, rope_sum, dq = [], None, []
        k_fulls = [jnp.concatenate([both[:, h * 256 : h * 256 + 128], all_keys[:, D_LAT:]], axis=1) for h in heads]
        values = [both[:, h * 256 + 128 : (h + 1) * 256] for h in heads]
        scores = [dot_nt(qf[h], k_fulls[h]) for h in heads]
        scores = [jnp.concatenate([jnp.where(shown, x[:, :TILE], HIDE), x[:, TILE:]], axis=1) for x in scores]
        dprobs = [dot_nt(gb[h], values[h]) for h in heads]
        expos = [jnp.exp2(x * base2 - jnp.max(x, axis=1, keepdims=True) * base2) for x in scores]
        invs = [1.0 / jnp.sum(x, axis=1, keepdims=True) for x in expos]
        expos = [x.astype(BF) for x in expos]
        mixes = [dot(expos[h], values[h]) * invs[h] for h in heads]
        gs = [gb[h].astype(F32) for h in heads]
        dvs = [dot((gs[h] * invs[h]).astype(BF).T, expos[h]) for h in heads]
        dss = []
        for h in heads:
            out[:, h * D_V : (h + 1) * D_V] = mixes[h].astype(BF)
            slope = invs[h] * SCALING
            offset = jnp.sum(mixes[h] * gs[h], axis=1, keepdims=True) * slope
            dss.append((expos[h].astype(F32) * (dprobs[h] * slope - offset)).astype(BF))
        dks = [dot(qt[h], dss[h]) for h in heads]
        dq = [dot(dss[h], k_fulls[h]) for h in heads]
        for h in heads:
            parts += [dks[h][:D_NOPE].astype(BF), dvs[h].astype(BF)]
        rope_sum = sum([x[D_NOPE:] for x in dks[1:]], dks[0][D_NOPE:])
        dkv = jnp.concatenate(parts, axis=0)
        add_grads(slice(0, width), dot(wt[...], dkv), rope_sum)
        finish_heads(dq, dot(dkv, all_keys[:, :D_LAT]))

    def loop_step():
        row = lax.broadcasted_iota(jnp.int32, (ROWS, TILE), 0)
        col = lax.broadcasted_iota(jnp.int32, (ROWS, TILE), 1)

        def score_tile(t, maxima):
            tile_keys = keys[key_rows(t), :]
            both = dot_nt(tile_keys[:, :D_LAT], wb[...]).astype(BF)
            shown = col <= row + t * (MAX_TILES * TILE)
            new = []
            for h in range(HEADS):
                k_nope = both[:, h * 256 : h * 256 + 128]
                value = both[:, h * 256 + 128 : (h + 1) * 256]
                k_full = jnp.concatenate([k_nope, tile_keys[:, D_LAT:]], axis=1)
                kf[h, t] = k_full
                vv[h, t] = value
                score = jnp.where(shown, dot_nt(qf[h], k_full), HIDE)
                s[h, t] = score
                dp[h, t] = dot_nt(gb[h], value)
                new.append(jnp.maximum(maxima[h], jnp.maximum(score[:, :128], score[:, 128:])))
            return tuple(new)

        low = jnp.full((ROWS, 128), HIDE, F32)
        maxima = each_tile(score_tile, (low,) * HEADS)
        shifts = [jnp.max(m, axis=1, keepdims=True) * base2 for m in maxima]

        def prob_tile(t, carry):
            new = []
            for h in range(HEADS):
                total, mixed = carry[h]
                expo = jnp.exp2(s[h, t] * base2 - shifts[h])
                total = total + (expo[:, :128] + expo[:, 128:])
                expo = expo.astype(BF)
                e[h, t] = expo
                new.append((total, mixed + dot(expo, vv[h, t])))
            return tuple(new)

        nothing = jnp.zeros((ROWS, 128), F32)
        mixes = each_tile(prob_tile, ((nothing, nothing),) * HEADS)
        slopes, offsets = [], []
        for h in range(HEADS):
            total, mixed = mixes[h]
            inv = 1.0 / jnp.sum(total, axis=1, keepdims=True)
            mixed = mixed * inv
            out[:, h * D_V : (h + 1) * D_V] = mixed.astype(BF)
            g = gb[h].astype(F32)
            row_dot = jnp.sum(mixed * g, axis=1, keepdims=True)
            slopes.append(inv * SCALING)
            offsets.append(row_dot * (inv * SCALING))
            git[h] = (g * inv).astype(BF).T

        wgrad[...] = jnp.zeros(wgrad.shape, F32)

        def back_tile(t, carry):
            tile_keys = keys[key_rows(t), :D_LAT]
            parts, rope_sum, new = [], None, []
            for h in range(HEADS):
                expo = e[h, t]
                ds = (expo.astype(F32) * (dp[h, t] * slopes[h] - offsets[h])).astype(BF)
                new.append(carry[h] + dot(ds, kf[h, t]))
                dk = dot(qt[h], ds)
                dv = dot(git[h], expo)
                parts += [dk[:D_NOPE].astype(BF), dv.astype(BF)]
                rope_sum = dk[D_NOPE:] if h == 0 else rope_sum + dk[D_NOPE:]
            dkv = jnp.concatenate(parts, axis=0)
            add_grads(key_rows(t), dot(wt[...], dkv), rope_sum)
            wgrad[...] += dot(dkv, tile_keys)
            return tuple(new)

        empty = jnp.zeros((ROWS, 256), F32)
        dq = each_tile(back_tile, (empty,) * HEADS)
        finish_heads(dq, wgrad[...])

    for count in WIDE:

        @pl.when(tiles == count)
        def _(count=count):
            wide_step(count)

    @pl.when(functools.reduce(lambda x, y: x & y, [tiles != count for count in WIDE]))
    def _():
        loop_step()

    @pl.when(step == pl.num_programs(0) - 1)
    def _():
        chunk, core = info[0], info[1]
        n1, block1, block2, count = meta[1], meta[2], meta[3], meta[4]
        kept[...] = jnp.zeros(kept.shape, BF)
        sent[...] = jnp.zeros(sent.shape, BF)

        def turn(t, carry):
            keys[key_rows(t), :D_LAT] = acc[:D_LAT, key_rows(t)].astype(BF).T
            keys[key_rows(t), D_LAT:] = jnp.concatenate(
                [acc[D_LAT:, key_rows(t)].astype(BF), jnp.zeros((EXTRA - D_ROPE, TILE), BF)], axis=0
            ).T
            return carry

        lax.fori_loop(0, tiles, turn, 0)

        def put(target, slot, y, index):
            target[slot, y] = keys[pl.ds(pl.multiple_of(index * BLOCK, BLOCK), BLOCK), :]

        own_blocks = ROWS // BLOCK
        for y in range(4):
            for target, parity in ((kept, core), (sent, 1 - core)):
                kind = 2 * y + parity
                for i in range(2):
                    put(target, i, y, 8 * i + kind)
                slot = 2
                for start, shift, length in ((block1, 0, n1), (block2, n1, count - n1)):
                    skip = (kind - start) & 7
                    number = jnp.maximum(length - skip + 7, 0) // 8

                    def put_next(i, carry, target=target, y=y, slot=slot, skip=skip, shift=shift):
                        put(target, slot + i, y, own_blocks + shift + skip + 8 * i)
                        return carry

                    lax.fori_loop(0, number, put_next, 0)
                    slot = slot + number


def attention(shared, q_nope, q_rope, d_out, w_uk, w_uv):
    rows = q_nope.shape[0]
    pairs = w_uk.shape[0] // (HEADS * D_NOPE)

    def columns(size):
        return pl.BlockSpec((rows, size), lambda i: (0, i))

    def heads(size):
        return pl.BlockSpec((size, D_LAT), lambda i: (i, 0))

    whole = pl.BlockSpec(memory_space=pltpu.VMEM)
    in_specs = [pl.BlockSpec(memory_space=pltpu.SMEM)] + [whole] * 5
    in_specs += [columns(HEADS * D_NOPE), columns(HEADS * D_ROPE), columns(HEADS * D_V), heads(HEADS * D_NOPE), heads(HEADS * D_V)]
    half = jax.ShapeDtypeStruct((SLOTS, 4, BLOCK, PACK), BF)
    return pl.pallas_call(
        attention_kernel,
        grid=(pairs,),
        in_specs=in_specs,
        out_specs=[
            columns(HEADS * D_V),
            columns(HEADS * D_NOPE),
            columns(HEADS * D_ROPE),
            pl.BlockSpec((HEADS, 256, D_LAT), lambda i: (i, 0, 0)),
            whole,
            whole,
            pl.BlockSpec(memory_space=pltpu.SMEM),
        ],
        out_shape=[
            jax.ShapeDtypeStruct(q_nope.shape, BF),
            jax.ShapeDtypeStruct(q_nope.shape, BF),
            jax.ShapeDtypeStruct(q_rope.shape, BF),
            jax.ShapeDtypeStruct((HEADS * pairs, 256, D_LAT), BF),
            half,
            half,
            jax.ShapeDtypeStruct((8,), jnp.int32),
        ],
        scratch_shapes=[
            pltpu.VMEM((MAX_TILES * TILE, PACK), BF),
            pltpu.VMEM((D_LAT + D_ROPE, MAX_TILES * TILE), F32),
            pltpu.VMEM((HEADS, MAX_TILES, TILE, 256), BF),
            pltpu.VMEM((HEADS, MAX_TILES, TILE, D_V), BF),
            pltpu.VMEM((HEADS, MAX_TILES, ROWS, TILE), F32),
            pltpu.VMEM((HEADS, MAX_TILES, ROWS, TILE), F32),
            pltpu.VMEM((HEADS, MAX_TILES, ROWS, TILE), BF),
            pltpu.VMEM((HEADS, ROWS, 256), BF),
            pltpu.VMEM((HEADS, D_NOPE + D_ROPE, ROWS), BF),
            pltpu.VMEM((HEADS, ROWS, D_V), BF),
            pltpu.VMEM((HEADS, D_V, ROWS), BF),
            pltpu.VMEM((HEADS * 256, D_LAT), BF),
            pltpu.VMEM((D_LAT, HEADS * 256), BF),
            pltpu.VMEM((HEADS * 256, D_LAT), F32),
        ],
        compiler_params=pltpu.CompilerParams(vmem_limit_bytes=56 << 20),
        cost_estimate=pl.CostEstimate(
            flops=pairs * HEADS * 1300000000, bytes_accessed=16 << 20, transcendentals=pairs * 400000
        ),
        name="attention",
    )(*shared, q_nope, q_rope, d_out, w_uk, w_uv)


def pack_rows(latent, gain, rope_t, gid, cid):
    latent_f = latent[...].astype(F32)
    inv = lax.rsqrt(jnp.mean(latent_f * latent_f, axis=1, keepdims=True) + 1e-06)
    normed = (latent_f * inv * gain[...].astype(F32)[None, :]).astype(BF)
    group = jnp.broadcast_to(gid[...].astype(F32), (8, ROWS)).T[:, :1].astype(jnp.int32)
    comp = jnp.broadcast_to(cid[...].astype(F32), (8, ROWS)).T[:, :1].astype(jnp.int32)
    code = group * (COMP + 1) + comp
    column = lax.broadcasted_iota(jnp.int32, (ROWS, EXTRA - D_ROPE), 1)
    tags = jnp.where(column == code, 1.0, 0.0).astype(BF)
    packed = jnp.concatenate([normed, rope_t[...].T, tags], axis=1)
    return packed, inv, group, comp, code, column


def pack_kernel(latent, gain, rope_t, gid, cid, send, own):
    core = lax.axis_index("core")
    own[...] = pack_rows(latent, gain, rope_t, gid, cid)[0]
    half = own[pl.ds(pl.multiple_of(core * (ROWS // 2), ROWS // 2), ROWS // 2), :]
    for i in range(CTX):
        send[i] = half


def pack(latent, latent_gain, k_rope_t, group_ids, comp_ids):
    vector = pl.BlockSpec(memory_space=LOCAL)
    return pl.pallas_call(
        pack_kernel,
        in_specs=[vector] * 5,
        out_specs=vector,
        out_shape=jax.ShapeDtypeStruct((CTX, ROWS // 2, PACK), BF),
        scratch_shapes=[pltpu.VMEM((ROWS, PACK), BF)],
        cost_estimate=SMALL,
        name="pack",
    )(latent, latent_gain, k_rope_t, group_ids[None, :], comp_ids[None, :])


def prepare_kernel(latent, gain, rope_t, gid, cid, gid_s, cid_s, lengths, own, bias, weight, inverse, info):
    packed, inv, group, comp, code, column = pack_rows(latent, gain, rope_t, gid, cid)
    own[...] = packed
    inverse[...] = inv
    seen = (column == code) | (column == group * (COMP + 1))
    bias[...] = jnp.where(seen, 0.0, HIDE).astype(BF)
    length = jnp.ones((ROWS, 1), F32)
    for g in range(GROUPS):
        for k in range(COMP):
            length = jnp.where(code == g * (COMP + 1) + k + 1, lengths[g, k].astype(F32), length)
    weight[...] = jnp.where(comp > 0, 64.0 / length, 0.0)
    group0, comp0 = gid_s[0], cid_s[0]
    info[0] = lax.axis_index("xl") * 4 + lax.axis_index("z")
    info[1], info[2], info[3] = lax.axis_index("core"), group0, comp0
    info[4] = jnp.sum(
        jnp.where(gid[...] * (COMP + 1) + cid[...] == group0 * (COMP + 1) + comp0, 1.0, 0.0)
    ).astype(jnp.int32)
    info[5] = lengths[group0, jnp.maximum(comp0 - 1, 0)]
    for g in range(GROUPS):
        info[6 + g] = sum([lengths[g, k] for k in range(1, COMP)], lengths[g, 0])


def prepare(latent, latent_gain, k_rope_t, group_ids, comp_ids, comp_lengths):
    vector = pl.BlockSpec(memory_space=LOCAL)
    scalar = pl.BlockSpec(memory_space=pltpu.SMEM)
    return pl.pallas_call(
        prepare_kernel,
        in_specs=[vector] * 5 + [scalar] * 3,
        out_specs=[vector] * 4 + [scalar],
        out_shape=[
            jax.ShapeDtypeStruct((ROWS, PACK), BF),
            jax.ShapeDtypeStruct((ROWS, EXTRA - D_ROPE), BF),
            jax.ShapeDtypeStruct((ROWS, 1), F32),
            jax.ShapeDtypeStruct((ROWS, 1), F32),
            jax.ShapeDtypeStruct((8,), jnp.int32),
        ],
        cost_estimate=LONG,
        name="prepare",
    )(
        latent,
        latent_gain,
        k_rope_t,
        group_ids[None, :],
        comp_ids[None, :],
        group_ids,
        comp_ids,
        comp_lengths,
    )


def move(x, axis, distance):
    if axis == "x":
        names = ("xl", "xh")
        return lax.ppermute(x, names, [(i, i ^ distance) for i in range(4)])
    return lax.ppermute(x, axis, [(i, (i + distance) % 4) for i in range(4)])


def summed(parts, index):
    total = parts[0][index].astype(F32)
    for part in parts[1:]:
        total = total + part[index].astype(F32)
    return total.astype(BF)


def fold_y_kernel(*refs):
    parts, outs = refs[:2], refs[2:]
    slots = outs[0].shape[0]
    for distance, out in enumerate(outs):
        place = (lax.axis_index("y") + distance) & 3
        for slot in range(slots):
            out[slot] = summed(parts, (slot, place))


def fold_z_kernel(*refs):
    meta, parts, outs = refs[0], refs[1:5], refs[5:9]
    n1, block1, block2, count, chunk = meta[1], meta[2], meta[3], meta[4], meta[5]
    kind = 2 * lax.axis_index("y") + lax.axis_index("core")
    z = lax.axis_index("z")
    spread = refs[9]
    spread[...] = jnp.zeros(spread.shape, BF)

    def put(slot, block):
        pair = block // 8
        spread[(((pair // 2) % 4) - z) & 3, (pair // 8) * 2 + pair % 2] = summed(parts, (slot,))

    for i in range(2):
        put(i, chunk * (ROWS // BLOCK) + 8 * i + kind)
    slot = 2
    for start, length in ((block1, n1), (block2, count - n1)):
        skip = (kind - start) & 7
        number = jnp.maximum(length - skip + 7, 0) // 8

        def put_next(i, carry, slot=slot, first=start + skip):
            put(slot + i, first + 8 * i)
            return carry

        lax.fori_loop(0, number, put_next, 0)
        slot = slot + number
    for distance, out in enumerate(outs):
        out[...] = spread[distance]


def fold(kernel, operands, cuts, shape, scratch=()):
    vector = pl.BlockSpec(memory_space=LOCAL)
    scalar = pl.BlockSpec(memory_space=pltpu.SMEM)
    return pl.pallas_call(
        kernel,
        in_specs=[scalar if x.dtype == jnp.int32 else vector for x in operands],
        out_specs=[vector] * cuts,
        out_shape=[jax.ShapeDtypeStruct(shape, BF)] * cuts,
        scratch_shapes=scratch,
        cost_estimate=LONG if kernel is fold_y_kernel else SMALL,
        name="fold",
    )(*operands)


def gather_grads(kept, sent, meta, total):
    slots = sent.shape[0]
    cut = fold(fold_y_kernel, [kept, swap_core(sent)], 4, (slots, BLOCK, PACK))
    parts = [cut[0]] + [move(cut[d], "y", d) for d in (2, 1, 3)]
    spread = pltpu.VMEM((4, 4, BLOCK, PACK), BF)
    cut = fold(fold_z_kernel, [meta] + parts, 4, (4, BLOCK, PACK), [spread])
    parts = [cut[0]] + [move(cut[d], "z", d) for d in (2, 1, 3)]
    parts, total = lax.optimization_barrier((parts, total))
    part = sum([x.astype(F32) for x in parts[1:]], parts[0].astype(F32)).astype(BF)
    part, total = lax.optimization_barrier((part, total))
    return total, [part] + [move(part, "x", d) for d in (1, 2, 3)]


def finish_kernel(a, b, c, d, latent, inverse, gain, out):
    head = lax.axis_index("y") * 2 + lax.axis_index("core")
    blocks = pl.ds(lax.axis_index("xl") * 2, 2)
    total = sum([part[blocks].astype(F32) for part in (b, c, d)], a[blocks].astype(F32))
    total = total.reshape(2 * BLOCK, PACK)
    lifted = total[:, :D_LAT] * gain[...].astype(F32)[None, :]
    places = [pl.ds(pl.multiple_of((xh * 8 + head) * BLOCK, BLOCK), BLOCK) for xh in range(2)]
    own = jnp.concatenate([latent[rows, :] for rows in places], axis=0).astype(F32)
    inv = jnp.concatenate([inverse[rows, :] for rows in places], axis=0)
    centred = jnp.mean(lifted * own, axis=1, keepdims=True)
    out[:, :D_LAT] = (inv * lifted - own * inv**3 * centred).astype(BF)
    out[:, D_LAT:] = total[:, D_LAT:].astype(BF)


def finish(parts, latent, inverse, latent_gain):
    vector = pl.BlockSpec(memory_space=LOCAL)
    return pl.pallas_call(
        finish_kernel,
        in_specs=[vector] * 7,
        out_specs=vector,
        out_shape=jax.ShapeDtypeStruct((2 * BLOCK, PACK), BF),
        cost_estimate=LONG,
        name="finish",
    )(*parts, latent, inverse, latent_gain)


def assemble_kernel(*refs):
    pieces, out, rope, turned = refs[:4], refs[4], refs[5], refs[6]
    y, core = lax.axis_index("y"), lax.axis_index("core")
    for distance, piece in enumerate(pieces):
        for other in range(2):
            for xh in range(2):
                head = xh * 8 + ((y - distance) & 3) * 2 + (core ^ other)
                rows = pl.ds(pl.multiple_of(head * BLOCK, BLOCK), BLOCK)
                place = (other * 2 + xh) * BLOCK
                out[rows, :] = piece[place : place + BLOCK, :D_LAT]
                turned[rows, :] = piece[place : place + BLOCK, D_LAT:].astype(F32)
    rope[...] = turned[...].T[:D_ROPE].astype(BF)


def assemble(pieces):
    vector = pl.BlockSpec(memory_space=LOCAL)
    return pl.pallas_call(
        assemble_kernel,
        in_specs=[vector] * 4,
        out_specs=[vector] * 2,
        out_shape=[
            jax.ShapeDtypeStruct((ROWS, D_LAT), BF),
            jax.ShapeDtypeStruct((D_ROPE, ROWS), BF),
        ],
        scratch_shapes=[pltpu.VMEM((ROWS, EXTRA), F32)],
        cost_estimate=SMALL,
        name="assemble",
    )(*pieces)


def total_kernel(pieces, out, parts, sums, in_sems, out_sems):
    steps = in_sems.shape[0]
    size = sums.shape[0] // steps
    copies = []

    def load(step):
        rows = pl.ds(step * size, size)
        return pltpu.make_async_copy(pieces.at[:, rows, :], parts.at[:, rows, :], in_sems.at[step])

    for step in range(steps):
        load(step).start()
    for step in range(steps):
        load(step).wait()
        rows = pl.ds(step * size, size)
        total = parts[0, rows, :].astype(F32)
        for i in range(1, CTX):
            total = total + parts[i, rows, :].astype(F32)
        sums[rows, :] = total.astype(BF)
        for i in range(CTX):
            copy = pltpu.make_async_copy(sums.at[rows, :], out.at[i, rows, :], out_sems.at[step, i])
            copy.start()
            copies.append(copy)
    for copy in copies:
        copy.wait()


def total_and_copy(pieces):
    anywhere = pl.BlockSpec(memory_space=pl.ANY)
    return pl.pallas_call(
        total_kernel,
        in_specs=[anywhere],
        out_specs=anywhere,
        out_shape=jax.ShapeDtypeStruct(pieces.shape, BF),
        scratch_shapes=[
            pltpu.VMEM(pieces.shape, BF),
            pltpu.VMEM(pieces.shape[1:], BF),
            pltpu.SemaphoreType.DMA((4,)),
            pltpu.SemaphoreType.DMA((4, CTX)),
        ],
        compiler_params=pltpu.CompilerParams(vmem_limit_bytes=62 << 20),
        cost_estimate=SMALL,
        name="total",
    )(pieces)


def swap_core(x):
    return lax.ppermute(x, "core", [(0, 1), (1, 0)])


def exchange(x, axes):
    return lax.all_to_all(x, axes, 0, 0, tiled=True)


def on_device(
    q_nope,
    q_rope,
    latent,
    latent_gain,
    k_rope_t,
    w_uk,
    w_uv,
    d_out,
    group_ids,
    comp_ids,
    comp_lengths,
):
    send = pack(latent, latent_gain, k_rope_t, group_ids, comp_ids)
    own, bias, weight, inverse, info = prepare(
        latent, latent_gain, k_rope_t, group_ids, comp_ids, comp_lengths
    )
    mine = exchange(send, CTX_AXES).reshape(-1, PACK)
    other = swap_core(mine)
    shared = (info, own, mine, other, bias, weight)
    out, dqn, dqr, dw, kept, sent, meta = attention(shared, q_nope, q_rope, d_out, w_uk, w_uv)
    pieces = exchange(dw, CTX_AXES)
    total = total_and_copy(pieces)
    total, parts = gather_grads(kept, sent, meta, total)
    weights = exchange(total, CTX_AXES)
    final = finish(parts, latent, inverse, latent_gain)
    pair = jnp.concatenate([final, swap_core(final)], axis=0)
    d_latent, d_k_rope_t = assemble([pair] + [move(pair, "y", d) for d in (1, 2, 3)])
    return out, dqn, dqr, d_latent, d_k_rope_t, *[
        weights[:, i * D_NOPE : (i + 1) * D_NOPE].reshape(-1, D_LAT) for i in range(2)
    ]


def solution(mesh):
    fine = Mesh(mesh.devices.reshape(2, 4, 2, 4, 2), CTX_AXES + HEAD_AXES)
    return jax.shard_map(
        on_device,
        mesh=fine,
        in_specs=(
            P(CTX_AXES, HEAD_AXES),
            P(CTX_AXES, HEAD_AXES),
            P(CTX_AXES, None),
            P(),
            P(None, CTX_AXES),
            P(HEAD_AXES, None),
            P(HEAD_AXES, None),
            P(CTX_AXES, HEAD_AXES),
            P(CTX_AXES),
            P(CTX_AXES),
            P(),
        ),
        out_specs=(
            P(CTX_AXES, HEAD_AXES),
            P(CTX_AXES, HEAD_AXES),
            P(CTX_AXES, HEAD_AXES),
            P(CTX_AXES, None),
            P(None, CTX_AXES),
            P(HEAD_AXES, None),
            P(HEAD_AXES, None),
        ),
        check_vma=False,
    )
```

```python
import functools
import math

import jax
import jax.numpy as jnp
from jax import lax
from jax.experimental import pallas as pl
from jax.experimental.pallas import tpu as pltpu
from jax.sharding import Mesh
from jax.sharding import PartitionSpec as P

D_LAT = 512
D_ROPE = 64
D_NOPE = 128
D_V = 128
GROUPS = 2
COMP = 8
CODES = GROUPS * (COMP + 1)
TOKENS = 2048
CTX = 8
ROWS = TOKENS // CTX
BLOCK = 16
TILE = 256
MAX_TILES = 6
HEADS = 4
SLOTS = 12
WIDE = (3, 4)
LONG = pl.CostEstimate(flops=100000000000, bytes_accessed=1, transcendentals=0)
SMALL = pl.CostEstimate(flops=1, bytes_accessed=1, transcendentals=0)
PACK = 640
EXTRA = PACK - D_LAT
PAD_COL = PACK - 1
HIDE = -1e30
SCALING = 1.0 / math.sqrt(D_NOPE + D_ROPE)
BF = jnp.bfloat16
F32 = jnp.float32
CTX_AXES = ("xl", "z")
HEAD_AXES = ("xh", "y", "core")
LOCAL = pltpu.VMEM


def dot(a, b):
    return lax.dot_general(a, b, (((1,), (0,)), ((), ())), preferred_element_type=F32)


def dot_nt(a, b):
    return lax.dot_general(a, b, (((1,), (1,)), ((), ())), preferred_element_type=F32)


def attention_kernel(*refs):
    info, own, mine, other, bias, weight, qn, qr, do, wk, wv = refs[:11]
    out, dqn, dqr, dw, kept, sent, meta = refs[11:18]
    keys, acc, kf, vv, s, dp, e, qf, qt, gb, git, wb, wt, wgrad = refs[18:]
    step = pl.program_id(0)

    def key_rows(t):
        return pl.ds(pl.multiple_of(t * TILE, TILE), TILE)

    @pl.when(step == 0)
    def _():
        chunk, core, group, comp = info[0], info[1], info[2], info[3]
        inside, length, len0, len1 = info[4], info[5], info[6], info[7]
        tags = jnp.sum(
            mine[:, D_LAT:].astype(F32) + other[:, D_LAT:].astype(F32), axis=0, keepdims=True
        )
        lane = lax.broadcasted_iota(jnp.int32, tags.shape, 1) - D_ROPE
        start1 = jnp.sum(jnp.where((lane >= 0) & (lane < COMP + 1), tags, 0.0)).astype(jnp.int32)
        begin = chunk * ROWS
        low1 = jnp.where(group == 0, 0, start1)
        high1 = jnp.minimum(jnp.where(group == 0, start1 - len0, TOKENS - len1), begin)
        block1 = low1 // BLOCK
        n1 = jnp.where(high1 > low1, (high1 + BLOCK - 1) // BLOCK - block1, 0)
        prior = jnp.where(comp > 0, length - inside, 0)
        block2 = jnp.maximum((begin - prior) // BLOCK, jnp.where(n1 > 0, block1 + n1, 0))
        count = n1 + jnp.maximum(begin // BLOCK - block2, 0)
        count = jnp.minimum(count, (MAX_TILES - 1) * (TILE // BLOCK))
        tiles = 1 + (count + TILE // BLOCK - 1) // (TILE // BLOCK)
        meta[0], meta[1], meta[2], meta[3], meta[4] = tiles, n1, block1, block2, count
        meta[5] = chunk
        keys[0:ROWS, :] = own[...]

        def copy_block(index, carry):
            block = jnp.where(index < n1, block1 + index, block2 + index - n1)
            place = (block // 16) * 8 + block % 8
            rows = pl.ds(pl.multiple_of(place * BLOCK, BLOCK), BLOCK)
            from_mine = ((block % 16) // 8 == core).astype(jnp.int32)
            keys[pl.ds(pl.multiple_of(ROWS + index * BLOCK, BLOCK), BLOCK), :] = jnp.where(
                from_mine == 1, mine[rows, :], other[rows, :]
            )
            return carry

        lax.fori_loop(0, count, copy_block, 0)
        filler = (lax.broadcasted_iota(jnp.int32, (BLOCK, PACK), 1) == PAD_COL).astype(F32).astype(BF)

        def pad_block(index, carry):
            keys[pl.ds(pl.multiple_of(ROWS + index * BLOCK, BLOCK), BLOCK), :] = filler
            return carry

        lax.fori_loop(count, (tiles - 1) * (TILE // BLOCK), pad_block, 0)

        def start_acc(t, carry):
            acc[:, key_rows(t)] = jnp.zeros((acc.shape[0], TILE), F32)
            return carry

        lax.fori_loop(0, tiles, start_acc, 0)

    tiles = meta[0]

    def each_tile(body, carry):
        return lax.fori_loop(0, tiles, body, carry)

    row_weight = weight[...]
    for h in range(HEADS):
        nope = qn[:, h * D_NOPE : (h + 1) * D_NOPE]
        rope = qr[:, h * D_ROPE : (h + 1) * D_ROPE]
        qf[h] = jnp.concatenate([nope, rope, bias[...]], axis=1)
        qt[h] = jnp.concatenate([nope.T, rope.T], axis=0)
        gb[h] = (do[:, h * D_V : (h + 1) * D_V].astype(F32) * row_weight).astype(BF)
        w_head = jnp.concatenate(
            [wk[h * D_NOPE : (h + 1) * D_NOPE, :], wv[h * D_V : (h + 1) * D_V, :]], axis=0
        )
        wb[h * 256 : (h + 1) * 256, :] = w_head
        wt[:, h * 256 : (h + 1) * 256] = w_head.T

    base2 = SCALING * math.log2(math.e)

    def add_grads(cols, lat_grads, rope_grads):
        acc[:D_LAT, cols] += lat_grads
        acc[D_LAT:, cols] += rope_grads

    def finish_heads(dq, grad):
        for h in range(HEADS):
            dqn[:, h * D_NOPE : (h + 1) * D_NOPE] = dq[h][:, :D_NOPE].astype(BF)
            dw[h] = grad[h * 256 : (h + 1) * 256].astype(BF)
        dqr[...] = jnp.concatenate(
            [dq[h][:, D_NOPE : D_NOPE + D_ROPE] for h in range(HEADS)], axis=1
        ).astype(BF)

    def wide_step(count):
        width = count * TILE
        all_keys = keys[:width, :]
        both = dot_nt(all_keys[:, :D_LAT], wb[...]).astype(BF)
        shown = lax.broadcasted_iota(jnp.int32, (ROWS, TILE), 1) <= lax.broadcasted_iota(
            jnp.int32, (ROWS, TILE), 0
        )
        heads = range(HEADS)
        parts, rope_sum, dq = [], None, []
        k_fulls = [jnp.concatenate([both[:, h * 256 : h * 256 + 128], all_keys[:, D_LAT:]], axis=1) for h in heads]
        values = [both[:, h * 256 + 128 : (h + 1) * 256] for h in heads]
        scores = [dot_nt(qf[h], k_fulls[h]) for h in heads]
        scores = [jnp.concatenate([jnp.where(shown, x[:, :TILE], HIDE), x[:, TILE:]], axis=1) for x in scores]
        dprobs = [dot_nt(gb[h], values[h]) for h in heads]
        expos = [jnp.exp2(x * base2 - jnp.max(x, axis=1, keepdims=True) * base2) for x in scores]
        invs = [1.0 / jnp.sum(x, axis=1, keepdims=True) for x in expos]
        expos = [x.astype(BF) for x in expos]
        mixes = [dot(expos[h], values[h]) * invs[h] for h in heads]
        gs = [gb[h].astype(F32) for h in heads]
        dvs = [dot((gs[h] * invs[h]).astype(BF).T, expos[h]) for h in heads]
        dss = []
        for h in heads:
            out[:, h * D_V : (h + 1) * D_V] = mixes[h].astype(BF)
            slope = invs[h] * SCALING
            offset = jnp.sum(mixes[h] * gs[h], axis=1, keepdims=True) * slope
            dss.append((expos[h].astype(F32) * (dprobs[h] * slope - offset)).astype(BF))
        dks = [dot(qt[h], dss[h]) for h in heads]
        dq = [dot(dss[h], k_fulls[h]) for h in heads]
        for h in heads:
            parts += [dks[h][:D_NOPE].astype(BF), dvs[h].astype(BF)]
        rope_sum = sum([x[D_NOPE:] for x in dks[1:]], dks[0][D_NOPE:])
        dkv = jnp.concatenate(parts, axis=0)
        add_grads(slice(0, width), dot(wt[...], dkv), rope_sum)
        finish_heads(dq, dot(dkv, all_keys[:, :D_LAT]))

    def loop_step():
        row = lax.broadcasted_iota(jnp.int32, (ROWS, TILE), 0)
        col = lax.broadcasted_iota(jnp.int32, (ROWS, TILE), 1)

        def score_tile(t, maxima):
            tile_keys = keys[key_rows(t), :]
            both = dot_nt(tile_keys[:, :D_LAT], wb[...]).astype(BF)
            shown = col <= row + t * (MAX_TILES * TILE)
            new = []
            for h in range(HEADS):
                k_nope = both[:, h * 256 : h * 256 + 128]
                value = both[:, h * 256 + 128 : (h + 1) * 256]
                k_full = jnp.concatenate([k_nope, tile_keys[:, D_LAT:]], axis=1)
                kf[h, t] = k_full
                vv[h, t] = value
                score = jnp.where(shown, dot_nt(qf[h], k_full), HIDE)
                s[h, t] = score
                dp[h, t] = dot_nt(gb[h], value)
                new.append(jnp.maximum(maxima[h], jnp.maximum(score[:, :128], score[:, 128:])))
            return tuple(new)

        low = jnp.full((ROWS, 128), HIDE, F32)
        maxima = each_tile(score_tile, (low,) * HEADS)
        shifts = [jnp.max(m, axis=1, keepdims=True) * base2 for m in maxima]

        def prob_tile(t, carry):
            new = []
            for h in range(HEADS):
                total, mixed = carry[h]
                expo = jnp.exp2(s[h, t] * base2 - shifts[h])
                total = total + (expo[:, :128] + expo[:, 128:])
                expo = expo.astype(BF)
                e[h, t] = expo
                new.append((total, mixed + dot(expo, vv[h, t])))
            return tuple(new)

        nothing = jnp.zeros((ROWS, 128), F32)
        mixes = each_tile(prob_tile, ((nothing, nothing),) * HEADS)
        slopes, offsets = [], []
        for h in range(HEADS):
            total, mixed = mixes[h]
            inv = 1.0 / jnp.sum(total, axis=1, keepdims=True)
            mixed = mixed * inv
            out[:, h * D_V : (h + 1) * D_V] = mixed.astype(BF)
            g = gb[h].astype(F32)
            row_dot = jnp.sum(mixed * g, axis=1, keepdims=True)
            slopes.append(inv * SCALING)
            offsets.append(row_dot * (inv * SCALING))
            git[h] = (g * inv).astype(BF).T

        wgrad[...] = jnp.zeros(wgrad.shape, F32)

        def back_tile(t, carry):
            tile_keys = keys[key_rows(t), :D_LAT]
            parts, rope_sum, new = [], None, []
            for h in range(HEADS):
                expo = e[h, t]
                ds = (expo.astype(F32) * (dp[h, t] * slopes[h] - offsets[h])).astype(BF)
                new.append(carry[h] + dot(ds, kf[h, t]))
                dk = dot(qt[h], ds)
                dv = dot(git[h], expo)
                parts += [dk[:D_NOPE].astype(BF), dv.astype(BF)]
                rope_sum = dk[D_NOPE:] if h == 0 else rope_sum + dk[D_NOPE:]
            dkv = jnp.concatenate(parts, axis=0)
            add_grads(key_rows(t), dot(wt[...], dkv), rope_sum)
            wgrad[...] += dot(dkv, tile_keys)
            return tuple(new)

        empty = jnp.zeros((ROWS, 256), F32)
        dq = each_tile(back_tile, (empty,) * HEADS)
        finish_heads(dq, wgrad[...])

    for count in WIDE:

        @pl.when(tiles == count)
        def _(count=count):
            wide_step(count)

    @pl.when(functools.reduce(lambda x, y: x & y, [tiles != count for count in WIDE]))
    def _():
        loop_step()

    @pl.when(step == pl.num_programs(0) - 1)
    def _():
        chunk, core = info[0], info[1]
        n1, block1, block2, count = meta[1], meta[2], meta[3], meta[4]
        kept[...] = jnp.zeros(kept.shape, BF)
        sent[...] = jnp.zeros(sent.shape, BF)

        def turn(t, carry):
            keys[key_rows(t), :D_LAT] = acc[:D_LAT, key_rows(t)].astype(BF).T
            keys[key_rows(t), D_LAT:] = jnp.concatenate(
                [acc[D_LAT:, key_rows(t)].astype(BF), jnp.zeros((EXTRA - D_ROPE, TILE), BF)], axis=0
            ).T
            return carry

        lax.fori_loop(0, tiles, turn, 0)

        def put(target, slot, y, index):
            target[slot, y] = keys[pl.ds(pl.multiple_of(index * BLOCK, BLOCK), BLOCK), :]

        own_blocks = ROWS // BLOCK
        for y in range(4):
            for target, parity in ((kept, core), (sent, 1 - core)):
                kind = 2 * y + parity
                for i in range(2):
                    put(target, i, y, 8 * i + kind)
                slot = 2
                for start, shift, length in ((block1, 0, n1), (block2, n1, count - n1)):
                    skip = (kind - start) & 7
                    number = jnp.maximum(length - skip + 7, 0) // 8

                    def put_next(i, carry, target=target, y=y, slot=slot, skip=skip, shift=shift):
                        put(target, slot + i, y, own_blocks + shift + skip + 8 * i)
                        return carry

                    lax.fori_loop(0, number, put_next, 0)
                    slot = slot + number


def attention(shared, q_nope, q_rope, d_out, w_uk, w_uv):
    rows = q_nope.shape[0]
    pairs = w_uk.shape[0] // (HEADS * D_NOPE)

    def columns(size):
        return pl.BlockSpec((rows, size), lambda i: (0, i))

    def heads(size):
        return pl.BlockSpec((size, D_LAT), lambda i: (i, 0))

    whole = pl.BlockSpec(memory_space=pltpu.VMEM)
    in_specs = [pl.BlockSpec(memory_space=pltpu.SMEM)] + [whole] * 5
    in_specs += [columns(HEADS * D_NOPE), columns(HEADS * D_ROPE), columns(HEADS * D_V), heads(HEADS * D_NOPE), heads(HEADS * D_V)]
    half = jax.ShapeDtypeStruct((SLOTS, 4, BLOCK, PACK), BF)
    return pl.pallas_call(
        attention_kernel,
        grid=(pairs,),
        in_specs=in_specs,
        out_specs=[
            columns(HEADS * D_V),
            columns(HEADS * D_NOPE),
            columns(HEADS * D_ROPE),
            pl.BlockSpec((HEADS, 256, D_LAT), lambda i: (i, 0, 0)),
            whole,
            whole,
            pl.BlockSpec(memory_space=pltpu.SMEM),
        ],
        out_shape=[
            jax.ShapeDtypeStruct(q_nope.shape, BF),
            jax.ShapeDtypeStruct(q_nope.shape, BF),
            jax.ShapeDtypeStruct(q_rope.shape, BF),
            jax.ShapeDtypeStruct((HEADS * pairs, 256, D_LAT), BF),
            half,
            half,
            jax.ShapeDtypeStruct((8,), jnp.int32),
        ],
        scratch_shapes=[
            pltpu.VMEM((MAX_TILES * TILE, PACK), BF),
            pltpu.VMEM((D_LAT + D_ROPE, MAX_TILES * TILE), F32),
            pltpu.VMEM((HEADS, MAX_TILES, TILE, 256), BF),
            pltpu.VMEM((HEADS, MAX_TILES, TILE, D_V), BF),
            pltpu.VMEM((HEADS, MAX_TILES, ROWS, TILE), F32),
            pltpu.VMEM((HEADS, MAX_TILES, ROWS, TILE), F32),
            pltpu.VMEM((HEADS, MAX_TILES, ROWS, TILE), BF),
            pltpu.VMEM((HEADS, ROWS, 256), BF),
            pltpu.VMEM((HEADS, D_NOPE + D_ROPE, ROWS), BF),
            pltpu.VMEM((HEADS, ROWS, D_V), BF),
            pltpu.VMEM((HEADS, D_V, ROWS), BF),
            pltpu.VMEM((HEADS * 256, D_LAT), BF),
            pltpu.VMEM((D_LAT, HEADS * 256), BF),
            pltpu.VMEM((HEADS * 256, D_LAT), F32),
        ],
        compiler_params=pltpu.CompilerParams(vmem_limit_bytes=56 << 20),
        cost_estimate=pl.CostEstimate(
            flops=pairs * HEADS * 1300000000, bytes_accessed=16 << 20, transcendentals=pairs * 400000
        ),
        name="attention",
    )(*shared, q_nope, q_rope, d_out, w_uk, w_uv)


def pack_rows(latent, gain, rope_t, gid, cid):
    latent_f = latent[...].astype(F32)
    inv = lax.rsqrt(jnp.mean(latent_f * latent_f, axis=1, keepdims=True) + 1e-06)
    normed = (latent_f * inv * gain[...].astype(F32)[None, :]).astype(BF)
    group = jnp.broadcast_to(gid[...].astype(F32), (8, ROWS)).T[:, :1].astype(jnp.int32)
    comp = jnp.broadcast_to(cid[...].astype(F32), (8, ROWS)).T[:, :1].astype(jnp.int32)
    code = group * (COMP + 1) + comp
    column = lax.broadcasted_iota(jnp.int32, (ROWS, EXTRA - D_ROPE), 1)
    tags = jnp.where(column == code, 1.0, 0.0).astype(BF)
    packed = jnp.concatenate([normed, rope_t[...].T, tags], axis=1)
    return packed, inv, group, comp, code, column


def pack_kernel(latent, gain, rope_t, gid, cid, send, own):
    core = lax.axis_index("core")
    own[...] = pack_rows(latent, gain, rope_t, gid, cid)[0]
    half = own[pl.ds(pl.multiple_of(core * (ROWS // 2), ROWS // 2), ROWS // 2), :]
    for i in range(CTX):
        send[i] = half


def pack(latent, latent_gain, k_rope_t, group_ids, comp_ids):
    vector = pl.BlockSpec(memory_space=LOCAL)
    return pl.pallas_call(
        pack_kernel,
        in_specs=[vector] * 5,
        out_specs=vector,
        out_shape=jax.ShapeDtypeStruct((CTX, ROWS // 2, PACK), BF),
        scratch_shapes=[pltpu.VMEM((ROWS, PACK), BF)],
        cost_estimate=SMALL,
        name="pack",
    )(latent, latent_gain, k_rope_t, group_ids[None, :], comp_ids[None, :])


def prepare_kernel(latent, gain, rope_t, gid, cid, gid_s, cid_s, lengths, own, bias, weight, inverse, info):
    packed, inv, group, comp, code, column = pack_rows(latent, gain, rope_t, gid, cid)
    own[...] = packed
    inverse[...] = inv
    seen = (column == code) | (column == group * (COMP + 1))
    bias[...] = jnp.where(seen, 0.0, HIDE).astype(BF)
    length = jnp.ones((ROWS, 1), F32)
    for g in range(GROUPS):
        for k in range(COMP):
            length = jnp.where(code == g * (COMP + 1) + k + 1, lengths[g, k].astype(F32), length)
    weight[...] = jnp.where(comp > 0, 64.0 / length, 0.0)
    group0, comp0 = gid_s[0], cid_s[0]
    info[0] = lax.axis_index("xl") * 4 + lax.axis_index("z")
    info[1], info[2], info[3] = lax.axis_index("core"), group0, comp0
    info[4] = jnp.sum(
        jnp.where(gid[...] * (COMP + 1) + cid[...] == group0 * (COMP + 1) + comp0, 1.0, 0.0)
    ).astype(jnp.int32)
    info[5] = lengths[group0, jnp.maximum(comp0 - 1, 0)]
    for g in range(GROUPS):
        info[6 + g] = sum([lengths[g, k] for k in range(1, COMP)], lengths[g, 0])


def prepare(latent, latent_gain, k_rope_t, group_ids, comp_ids, comp_lengths):
    vector = pl.BlockSpec(memory_space=LOCAL)
    scalar = pl.BlockSpec(memory_space=pltpu.SMEM)
    return pl.pallas_call(
        prepare_kernel,
        in_specs=[vector] * 5 + [scalar] * 3,
        out_specs=[vector] * 4 + [scalar],
        out_shape=[
            jax.ShapeDtypeStruct((ROWS, PACK), BF),
            jax.ShapeDtypeStruct((ROWS, EXTRA - D_ROPE), BF),
            jax.ShapeDtypeStruct((ROWS, 1), F32),
            jax.ShapeDtypeStruct((ROWS, 1), F32),
            jax.ShapeDtypeStruct((8,), jnp.int32),
        ],
        cost_estimate=LONG,
        name="prepare",
    )(
        latent,
        latent_gain,
        k_rope_t,
        group_ids[None, :],
        comp_ids[None, :],
        group_ids,
        comp_ids,
        comp_lengths,
    )


def move(x, axis, distance):
    if axis == "x":
        names = ("xl", "xh")
        return lax.ppermute(x, names, [(i, i ^ distance) for i in range(4)])
    return lax.ppermute(x, axis, [(i, (i + distance) % 4) for i in range(4)])


def summed(parts, index):
    total = parts[0][index].astype(F32)
    for part in parts[1:]:
        total = total + part[index].astype(F32)
    return total.astype(BF)


def fold_y_kernel(*refs):
    parts, outs = refs[:2], refs[2:]
    slots = outs[0].shape[0]
    for distance, out in enumerate(outs):
        place = (lax.axis_index("y") + distance) & 3
        for slot in range(slots):
            out[slot] = summed(parts, (slot, place))


def fold_z_kernel(*refs):
    meta, parts, outs = refs[0], refs[1:5], refs[5:9]
    n1, block1, block2, count, chunk = meta[1], meta[2], meta[3], meta[4], meta[5]
    kind = 2 * lax.axis_index("y") + lax.axis_index("core")
    z = lax.axis_index("z")
    spread = refs[9]
    spread[...] = jnp.zeros(spread.shape, BF)

    def put(slot, block):
        pair = block // 8
        spread[(((pair // 2) % 4) - z) & 3, (pair // 8) * 2 + pair % 2] = summed(parts, (slot,))

    for i in range(2):
        put(i, chunk * (ROWS // BLOCK) + 8 * i + kind)
    slot = 2
    for start, length in ((block1, n1), (block2, count - n1)):
        skip = (kind - start) & 7
        number = jnp.maximum(length - skip + 7, 0) // 8

        def put_next(i, carry, slot=slot, first=start + skip):
            put(slot + i, first + 8 * i)
            return carry

        lax.fori_loop(0, number, put_next, 0)
        slot = slot + number
    for distance, out in enumerate(outs):
        out[...] = spread[distance]


def fold(kernel, operands, cuts, shape, scratch=()):
    vector = pl.BlockSpec(memory_space=LOCAL)
    scalar = pl.BlockSpec(memory_space=pltpu.SMEM)
    return pl.pallas_call(
        kernel,
        in_specs=[scalar if x.dtype == jnp.int32 else vector for x in operands],
        out_specs=[vector] * cuts,
        out_shape=[jax.ShapeDtypeStruct(shape, BF)] * cuts,
        scratch_shapes=scratch,
        cost_estimate=LONG if kernel is fold_y_kernel else SMALL,
        name="fold",
    )(*operands)


def gather_grads(kept, sent, meta, total):
    slots = sent.shape[0]
    cut = fold(fold_y_kernel, [kept, swap_core(sent)], 4, (slots, BLOCK, PACK))
    parts = [cut[0]] + [move(cut[d], "y", d) for d in (1, 3, 2)]
    spread = pltpu.VMEM((4, 4, BLOCK, PACK), BF)
    cut = fold(fold_z_kernel, [meta] + parts, 4, (4, BLOCK, PACK), [spread])
    parts = [cut[0]] + [move(cut[d], "z", d) for d in (1, 3, 2)]
    parts, total = lax.optimization_barrier((parts, total))
    part = sum([x.astype(F32) for x in parts[1:]], parts[0].astype(F32)).astype(BF)
    part, total = lax.optimization_barrier((part, total))
    return total, [part] + [move(part, "x", d) for d in (1, 2, 3)]


def finish_kernel(a, b, c, d, latent, inverse, gain, out):
    head = lax.axis_index("y") * 2 + lax.axis_index("core")
    blocks = pl.ds(lax.axis_index("xl") * 2, 2)
    total = sum([part[blocks].astype(F32) for part in (b, c, d)], a[blocks].astype(F32))
    total = total.reshape(2 * BLOCK, PACK)
    lifted = total[:, :D_LAT] * gain[...].astype(F32)[None, :]
    places = [pl.ds(pl.multiple_of((xh * 8 + head) * BLOCK, BLOCK), BLOCK) for xh in range(2)]
    own = jnp.concatenate([latent[rows, :] for rows in places], axis=0).astype(F32)
    inv = jnp.concatenate([inverse[rows, :] for rows in places], axis=0)
    centred = jnp.mean(lifted * own, axis=1, keepdims=True)
    out[:, :D_LAT] = (inv * lifted - own * inv**3 * centred).astype(BF)
    out[:, D_LAT:] = total[:, D_LAT:].astype(BF)


def finish(parts, latent, inverse, latent_gain):
    vector = pl.BlockSpec(memory_space=LOCAL)
    return pl.pallas_call(
        finish_kernel,
        in_specs=[vector] * 7,
        out_specs=vector,
        out_shape=jax.ShapeDtypeStruct((2 * BLOCK, PACK), BF),
        cost_estimate=LONG,
        name="finish",
    )(*parts, latent, inverse, latent_gain)


def assemble_kernel(*refs):
    pieces, out, rope, turned = refs[:4], refs[4], refs[5], refs[6]
    y, core = lax.axis_index("y"), lax.axis_index("core")
    for distance, piece in enumerate(pieces):
        for other in range(2):
            for xh in range(2):
                head = xh * 8 + ((y - distance) & 3) * 2 + (core ^ other)
                rows = pl.ds(pl.multiple_of(head * BLOCK, BLOCK), BLOCK)
                place = (other * 2 + xh) * BLOCK
                out[rows, :] = piece[place : place + BLOCK, :D_LAT]
                turned[rows, :] = piece[place : place + BLOCK, D_LAT:].astype(F32)
    rope[...] = turned[...].T[:D_ROPE].astype(BF)


def assemble(pieces):
    vector = pl.BlockSpec(memory_space=LOCAL)
    return pl.pallas_call(
        assemble_kernel,
        in_specs=[vector] * 4,
        out_specs=[vector] * 2,
        out_shape=[
            jax.ShapeDtypeStruct((ROWS, D_LAT), BF),
            jax.ShapeDtypeStruct((D_ROPE, ROWS), BF),
        ],
        scratch_shapes=[pltpu.VMEM((ROWS, EXTRA), F32)],
        cost_estimate=SMALL,
        name="assemble",
    )(*pieces)


def total_kernel(pieces, out, parts, sums, in_sems, out_sems):
    steps = in_sems.shape[0]
    size = sums.shape[0] // steps
    copies = []

    def load(step):
        rows = pl.ds(step * size, size)
        return pltpu.make_async_copy(pieces.at[:, rows, :], parts.at[:, rows, :], in_sems.at[step])

    for step in range(steps):
        load(step).start()
    for step in range(steps):
        load(step).wait()
        rows = pl.ds(step * size, size)
        total = parts[0, rows, :].astype(F32)
        for i in range(1, CTX):
            total = total + parts[i, rows, :].astype(F32)
        sums[rows, :] = total.astype(BF)
        for i in range(CTX):
            copy = pltpu.make_async_copy(sums.at[rows, :], out.at[i, rows, :], out_sems.at[step, i])
            copy.start()
            copies.append(copy)
    for copy in copies:
        copy.wait()


def total_and_copy(pieces):
    anywhere = pl.BlockSpec(memory_space=pl.ANY)
    return pl.pallas_call(
        total_kernel,
        in_specs=[anywhere],
        out_specs=anywhere,
        out_shape=jax.ShapeDtypeStruct(pieces.shape, BF),
        scratch_shapes=[
            pltpu.VMEM(pieces.shape, BF),
            pltpu.VMEM(pieces.shape[1:], BF),
            pltpu.SemaphoreType.DMA((4,)),
            pltpu.SemaphoreType.DMA((4, CTX)),
        ],
        compiler_params=pltpu.CompilerParams(vmem_limit_bytes=62 << 20),
        cost_estimate=SMALL,
        name="total",
    )(pieces)


def swap_core(x):
    return lax.ppermute(x, "core", [(0, 1), (1, 0)])


def exchange(x, axes):
    return lax.all_to_all(x, axes, 0, 0, tiled=True)


def on_device(
    q_nope,
    q_rope,
    latent,
    latent_gain,
    k_rope_t,
    w_uk,
    w_uv,
    d_out,
    group_ids,
    comp_ids,
    comp_lengths,
):
    send = pack(latent, latent_gain, k_rope_t, group_ids, comp_ids)
    own, bias, weight, inverse, info = prepare(
        latent, latent_gain, k_rope_t, group_ids, comp_ids, comp_lengths
    )
    mine = exchange(send, CTX_AXES).reshape(-1, PACK)
    other = swap_core(mine)
    shared = (info, own, mine, other, bias, weight)
    out, dqn, dqr, dw, kept, sent, meta = attention(shared, q_nope, q_rope, d_out, w_uk, w_uv)
    pieces = exchange(dw, CTX_AXES)
    total = total_and_copy(pieces)
    total, parts = gather_grads(kept, sent, meta, total)
    weights = exchange(total, CTX_AXES)
    final = finish(parts, latent, inverse, latent_gain)
    pair = jnp.concatenate([final, swap_core(final)], axis=0)
    d_latent, d_k_rope_t = assemble([pair] + [move(pair, "y", d) for d in (1, 2, 3)])
    return out, dqn, dqr, d_latent, d_k_rope_t, *[
        weights[:, i * D_NOPE : (i + 1) * D_NOPE].reshape(-1, D_LAT) for i in range(2)
    ]


def solution(mesh):
    fine = Mesh(mesh.devices.reshape(2, 4, 2, 4, 2), CTX_AXES + HEAD_AXES)
    return jax.shard_map(
        on_device,
        mesh=fine,
        in_specs=(
            P(CTX_AXES, HEAD_AXES),
            P(CTX_AXES, HEAD_AXES),
            P(CTX_AXES, None),
            P(),
            P(None, CTX_AXES),
            P(HEAD_AXES, None),
            P(HEAD_AXES, None),
            P(CTX_AXES, HEAD_AXES),
            P(CTX_AXES),
            P(CTX_AXES),
            P(),
        ),
        out_specs=(
            P(CTX_AXES, HEAD_AXES),
            P(CTX_AXES, HEAD_AXES),
            P(CTX_AXES, HEAD_AXES),
            P(CTX_AXES, None),
            P(None, CTX_AXES),
            P(HEAD_AXES, None),
            P(HEAD_AXES, None),
        ),
        check_vma=False,
    )
```
